32 devices in a mesh: wave: 4 (over z), lat: 8 (over y, x, core).
Axes of the slice: x: 2, y: 2, z: 4, core: 2. Of those that a mesh axis runs over, the one named last changes fastest.
Arguments:
- spectral: bfloat16 [2, 16, 131328], P(None, None, 'wave'), may hold values from -6 to 6
- legendre: bfloat16 [32, 131328], P('lat', 'wave'), may hold values from -0.375 to 0.375
- wave_of_slot: int32 [512], replicated, may hold values from 3488 to 3999, as said below
- row_points: int32 [8, 4], P('lat'), may hold values from 20 to 16016, as said below
- quad_weight: float32 [8, 4], P('lat'), may hold values from 0.2 to 1
- grid_factor: float32 [8, 4, 16016], P('lat'), may hold values from 0.5 to 2
Outputs:
- spectral_out: float32 [2, 16, 131328], P(None, None, 'wave')
The draws below stay inside these ranges and needn't reach their ends.
Inputs may be any that keep to these rules, and one draw needn't show every extreme that they name: `wave_of_slot`: slots 2 q and 2 q + 1 hold the wavenumbers 3488 + k and 3999 - k for one k of 0 to 255, each k once, so every owner holds 64 such pairs. `row_points`: each row has 20 + 4 min(i, 7999 - i) points for a latitude index i of the grid, the indices distinct over the rows; some row has 16016 points.
All inputs are finite; a program needn't handle non-finite values.
Results may differ from the reference program's by a relative error of at most 0.0024.
Values may be sent and summed in bfloat16 or wider, within the bound.
A program may use at most 64 MiB of HBM per device.

```python
import math
import jax
import jax.numpy as jnp
from jax import lax

TRUNC = 3999
M0 = 3488
MS = 512
NLAT = 8000
LEVELS = 16
NLON = 16016
NPACK = 131328
NROWS = 32
N_WAVE = 4
N_LAT = 8


def draw_wave_of_slot(key, part):
    key = jax.random.fold_in(key, 11)
    order = jax.random.permutation(key, MS // 2).astype(jnp.int32)
    lower = M0 + order
    upper = M0 + MS - 1 - order
    return jnp.stack([lower, upper], axis=1).reshape(MS).astype(jnp.int32)


def draw_row_points(key, part):
    key = jax.random.fold_in(key, 23)
    first_key, second_key = jax.random.split(key)
    middle = NLAT // 2 - 1
    picked = jax.random.permutation(first_key, NLAT - 1)[:NROWS - 1].astype(jnp.int32)
    picked = jnp.where(picked >= middle, picked + 1, picked)
    latitudes = jnp.concatenate([picked, jnp.full((1,), middle, jnp.int32)])
    latitudes = latitudes[jax.random.permutation(second_key, NROWS)]
    points = 20 + 4 * jnp.minimum(latitudes, NLAT - 1 - latitudes)
    return points.reshape(N_LAT, N_WAVE).astype(jnp.int32)


def block_levels(own_key, shape, pieces, least, largest):
    def one(axis_at, shards_of):
        heights = jax.random.uniform(jax.random.fold_in(jax.random.fold_in(own_key, 6), axis_at), (shards_of,), jnp.float32, least / len(pieces), largest / len(pieces))
        return jnp.repeat(jnp.exp(heights), shape[axis_at] // shards_of).reshape((-1,) + (1,) * (len(shape) - axis_at - 1))

    factor_of = one(*pieces[0])
    for cut in pieces[1:]:
        factor_of = factor_of * one(*cut)
    return factor_of


def bell_draw(key, dims, scale, most, pieces=(), held_as=jnp.bfloat16):
    loudness = block_levels(key, dims, pieces, -0.22, 0.18) if pieces else 1.0
    entries = jax.random.normal(key, dims, jnp.float32) * scale * loudness
    return jnp.minimum(jnp.maximum(entries, -most), most).astype(held_as)


def setup_inputs(seed: int = 0) -> dict:
    splits = jax.random.split(jax.random.key(seed), 7)
    return {
        "spectral": bell_draw(splits[0], (2, LEVELS, NPACK), 1.0, 6.0, ((2, 4),)),
        "legendre": bell_draw(splits[1], (NROWS, NPACK), 256 ** -0.5, 0.375, ((0, 8), (1, 4))),
        "wave_of_slot": draw_wave_of_slot(jax.random.fold_in(splits[6], 71), 0),
        "row_points": draw_row_points(jax.random.fold_in(splits[6], 71), 0),
        "quad_weight": jnp.clip(0.2 + 0.8 * jax.random.uniform(splits[4], (N_LAT, N_WAVE), jnp.float32) ** block_levels(splits[4], (N_LAT, N_WAVE), ((0, 8),), -0.2, 0.2), 0.2, 1.0),
        "grid_factor": jnp.clip(0.5 + 1.5 * jax.random.uniform(splits[5], (N_LAT, N_WAVE, NLON), jnp.float32) ** block_levels(splits[5], (N_LAT, N_WAVE, NLON), ((0, 8),), -0.2, 0.2), 0.5, 2.0),
    }


def phase_tables(count, start, length, limit, first, inner, outer):
    k = start + jnp.arange(length, dtype=jnp.int32)
    valid = k < limit

    def table(mult):
        turns = (mult[:, None] * k[None, :]) % count
        angle = turns.astype(jnp.float32) * (2.0 * math.pi) / count.astype(jnp.float32)
        return jnp.where(valid[None, :], jnp.cos(angle), 0.0), jnp.where(valid[None, :], jnp.sin(angle), 0.0)

    inner_cos, inner_sin = table(jnp.arange(inner, dtype=jnp.int32))
    outer_cos, outer_sin = table(first + inner * jnp.arange(outer, dtype=jnp.int32))
    return inner_cos, inner_sin, outer_cos, outer_sin


def synthesize(real_part, imag_part, tables):
    inner_cos, inner_sin, outer_cos, outer_sin = tables
    outer = outer_cos.shape[0]
    inner = inner_cos.shape[0]
    width = inner_cos.shape[1]
    levels = real_part.shape[1]
    stacked = jnp.concatenate([real_part.reshape(outer, inner, levels), imag_part.reshape(outer, inner, levels)], axis=1)
    left = stacked.transpose(0, 2, 1).reshape(outer * levels, 2 * inner)
    right = jnp.concatenate([jnp.concatenate([inner_cos, inner_sin], 1), jnp.concatenate([-inner_sin, inner_cos], 1)], 0)
    mixed = jnp.dot(left, right, precision=lax.Precision.HIGH, preferred_element_type=jnp.float32)
    part_re = mixed[:, :width].reshape(outer, levels, width)
    part_im = mixed[:, width:].reshape(outer, levels, width)
    return jnp.sum(part_re * outer_cos[:, None, :] - part_im * outer_sin[:, None, :], axis=0)


def analyse(field, tables):
    inner_cos, inner_sin, outer_cos, outer_sin = tables
    outer = outer_cos.shape[0]
    inner = inner_cos.shape[0]
    width = inner_cos.shape[1]
    levels = field.shape[0]
    rotated_re = field[None, :, :] * outer_cos[:, None, :]
    rotated_im = -field[None, :, :] * outer_sin[:, None, :]
    left = jnp.concatenate([rotated_re, rotated_im], axis=2).reshape(outer * levels, 2 * width)
    right = jnp.concatenate([jnp.concatenate([inner_cos.T, -inner_sin.T], 1), jnp.concatenate([inner_sin.T, inner_cos.T], 1)], 0)
    mixed = jnp.dot(left, right, precision=lax.Precision.HIGH, preferred_element_type=jnp.float32)
    coef_re = mixed[:, :inner].reshape(outer, levels, inner).transpose(0, 2, 1).reshape(outer * inner, levels)
    coef_im = mixed[:, inner:].reshape(outer, levels, inner).transpose(0, 2, 1).reshape(outer * inner, levels)
    return coef_re, coef_im


def reference(spectral, legendre, wave_of_slot, row_points, quad_weight, grid_factor):
    levels = spectral.shape[1]
    chans = 2 * levels
    own = NPACK // N_WAVE
    per_owner = MS // N_WAVE
    lengths = (TRUNC + 1 - wave_of_slot).reshape(N_WAVE, per_owner)
    ends = jnp.cumsum(lengths, axis=1).astype(jnp.int32)
    column_index = jnp.arange(NPACK, dtype=jnp.int32)
    owner = column_index // own
    local = column_index % own
    slot_of = (owner * per_owner + jnp.sum((local[:, None] >= ends[owner]).astype(jnp.int32), axis=1)).astype(jnp.int32)
    coeffs = spectral.reshape(chans, NPACK).astype(jnp.float32).T
    position = (wave_of_slot - M0).astype(jnp.int32)
    rows = legendre.shape[0]
    points = row_points.reshape(rows)
    weights = quad_weight.reshape(rows)
    factors = grid_factor.reshape(rows, NLON)

    def one_row(items):
        column, count, weight, factor = items
        terms = column.astype(jnp.float32)[:, None] * coeffs
        fourier = jax.ops.segment_sum(terms, slot_of, num_segments=MS).astype(jnp.bfloat16)
        by_wave = jnp.zeros((MS, chans), jnp.float32).at[position].set(fourier.astype(jnp.float32))
        tables = phase_tables(count, 0, NLON, count, M0, 32, MS // 32)
        field = synthesize(by_wave[:, :levels], by_wave[:, levels:], tables)
        coef_re, coef_im = analyse(field * factor[None, :], tables)
        scale = weight / count.astype(jnp.float32)
        back = (jnp.concatenate([coef_re, coef_im], 1) * scale).astype(jnp.bfloat16)
        return back[position]

    returned = lax.map(one_row, (legendre, points, weights, factors))

    def accumulate(total, items):
        column, back = items
        return total + column.astype(jnp.float32)[:, None] * back[slot_of].astype(jnp.float32), None

    total, unused = lax.scan(accumulate, jnp.zeros((NPACK, chans), jnp.float32), (legendre, returned))
    return total.T.reshape(2, levels, NPACK)
```

```python
import functools
import math

import jax
import jax.numpy as jnp
from jax import lax
from jax.experimental import pallas as pl
from jax.experimental.pallas import tpu as pltpu
from jax.sharding import PartitionSpec as P

TRUNC = 3999
M0 = 3488
MS = 512

F32 = jnp.float32
BF16 = jnp.bfloat16
RADIX = 4
CHUNK = 512


def dot(a, b, ca, cb):
    return lax.dot_general(a, b, (((ca,), (cb,)), ((), ())), preferred_element_type=F32)


def column_bounds(waves, first_slot, span):
    slot = first_slot + lax.broadcasted_iota(jnp.int32, waves.shape, 0)
    pair = slot // 2
    length = TRUNC + 1 - waves
    low = slot % 2 == 0
    begin = jnp.where(low, pair * span, (pair + 1) * span - length)
    end = jnp.where(low, pair * span + length, (pair + 1) * span)
    return begin, end


def fourier_kernel(span, waves_ref, spec_ref, leg_ref, out_ref):
    group, own = leg_ref.shape
    slots = waves_ref.shape[0]
    for first in range(0, slots, 8):
        c0 = first // 2 * span // 128 * 128
        c1 = min(-(-((first // 2 + 4) * span) // 128) * 128, own)
        begin, end = column_bounds(waves_ref[first : first + 8, :], first, span)
        column = c0 + lax.broadcasted_iota(jnp.int32, (8, c1 - c0), 1)
        inside = (column >= begin) & (column < end)
        rows = leg_ref[:, c0:c1].astype(F32)
        masked = jnp.concatenate(
            [jnp.where(inside, rows[r : r + 1, :], 0.0) for r in range(group)], 0
        ).astype(BF16)
        sums = dot(masked, spec_ref[:, c0:c1], 1, 1)
        for r in range(group):
            out_ref[r, first : first + 8, :] = sums[8 * r : 8 * r + 8, :].astype(BF16)


def output_kernel(span, waves_ref, leg_ref, back_ref, out_ref):
    rows, own = leg_ref.shape
    slots = waves_ref.shape[0]
    pairs = slots // 2
    for c0 in range(0, own, CHUNK):
        c1 = min(c0 + CHUNK, own)
        p0, p1 = c0 // span, (c1 - 1) // span + 1
        column = c0 + lax.broadcasted_iota(jnp.int32, (1, c1 - c0), 1)
        part = leg_ref[:, c0:c1].astype(F32)
        masked = []
        for pair in range(p0, p1):
            split = pair * span + TRUNC + 1 - waves_ref[2 * pair : 2 * pair + 1, :]
            low = (column >= pair * span) & (column < split)
            high = (column >= split) & (column < (pair + 1) * span)
            masked.append(jnp.where(low, part, 0.0))
            masked.append(jnp.where(high, part, 0.0))
        right = jnp.concatenate(masked, 0).astype(BF16)
        out_ref[:, c0:c1] = dot(back_ref[2 * p0 * rows : 2 * p1 * rows, :], right, 0, 0)


def sine_turns(v):
    y = v * v
    total = jnp.full_like(v, -((2 * math.pi) ** 11) / math.factorial(11))
    for power in (9, 7, 5, 3, 1):
        sign = 1.0 if power % 4 == 1 else -1.0
        total = total * y + sign * (2 * math.pi) ** power / math.factorial(power)
    return total * v


def angle_rows(count, start, width):
    row = lax.broadcasted_iota(jnp.int32, (32, width), 0)
    k = start + lax.broadcasted_iota(jnp.int32, (32, width), 1)
    mult = jnp.where(row < 8, M0 + 64 * row, jnp.where(row < 24, 4 * (row - 8), row - 24))
    product = (mult * k).astype(F32)
    inverse = 1.0 / count
    rest = product - count * jnp.round(product * inverse)
    turn = rest * inverse
    size = jnp.abs(turn)
    folded = jnp.minimum(size, 0.5 - size)
    return sine_turns(0.25 - size), jnp.where(turn < 0, -1.0, 1.0) * sine_turns(folded)


def halves(x):
    high = x.astype(BF16)
    return high, (x - high.astype(F32)).astype(BF16)


def order_matrix(waves):
    each = MS // RADIX
    column = lax.broadcasted_iota(jnp.int32, (MS, MS), 1)
    wave = M0 + RADIX * (column % each) + column // each
    return (waves == wave).astype(F32).astype(BF16)


def transform_kernel(info_ref, waves_ref, coef_ref, factor_ref, out_ref, acc_ref):
    count = info_ref[0]
    scale = info_ref[1]
    quarter = count * 0.25
    levels = coef_ref.shape[1] // 2
    each = MS // RADIX
    order = order_matrix(waves_ref[...])
    ordered = dot(coef_ref[...], order, 0, 0)
    real = [ordered[:levels, each * c : each * (c + 1)] for c in range(RADIX)]
    imag = [ordered[levels:, each * c : each * (c + 1)] for c in range(RADIX)]
    left = jnp.concatenate(
        [jnp.concatenate([real[c], -imag[c]], 1) for c in range(RADIX)]
        + [jnp.concatenate([imag[c], real[c]], 1) for c in range(1, RADIX)],
        0,
    ).astype(BF16)
    acc_ref[...] = jnp.zeros_like(acc_ref)

    def step(index, carry):
        start = index * CHUNK
        cos, sin = angle_rows(count, start, CHUNK)
        cos_b, sin_b = cos[8:24], sin[8:24]
        table = jnp.concatenate(
            [cos[a : a + 1] * cos_b - sin[a : a + 1] * sin_b for a in range(8)]
            + [sin[a : a + 1] * cos_b + cos[a : a + 1] * sin_b for a in range(8)],
            0,
        )
        high, low = halves(table)
        mixed = dot(left, high, 1, 0) + dot(left, low, 1, 0)
        h = [mixed[levels * i : levels * (i + 1)] for i in range(7)]
        c1, c2, c3 = cos[25:26], cos[26:27], cos[27:28]
        s1, s2, s3 = sin[25:26], sin[26:27], sin[27:28]
        re1, im1 = h[1] * c1 - h[4] * s1, h[1] * s1 + h[4] * c1
        re2 = h[2] * c2 - h[5] * s2
        re3, im3 = h[3] * c3 - h[6] * s3, h[3] * s3 + h[6] * c3
        e, f, p, d = h[0] + re2, h[0] - re2, re1 + re3, im1 - im3
        k = (start + lax.broadcasted_iota(jnp.int32, (1, CHUNK), 1)).astype(F32)
        g = jnp.where(k < quarter, factor_ref[:, pl.ds(pl.multiple_of(start, CHUNK), CHUNK)], 0.0)
        q0, q1, q2, q3 = g[0:1] * (e + p), g[1:2] * (f - d), g[2:3] * (e - p), g[3:4] * (f + d)
        x, y = q0 - q2, q1 - q3
        u, v = q0 + q2, q1 + q3
        w = u - v
        turned = jnp.concatenate(
            [
                u + v,
                x * c1 - y * s1,
                w * c2,
                x * c3 + y * s3,
                -(x * s1 + y * c1),
                -(w * s2),
                y * c3 - x * s3,
            ],
            0,
        )
        t_high, t_low = halves(turned)
        acc_ref[...] += dot(t_high, high, 1, 1) + dot(t_low, high, 1, 1) + dot(t_high, low, 1, 1)
        return carry

    lax.fori_loop(0, factor_ref.shape[1] // CHUNK, step, 0)
    total = acc_ref[...] * scale
    on_cos = [total[levels * i : levels * (i + 1), :each] for i in range(7)]
    on_sin = [total[levels * i : levels * (i + 1), each:] for i in range(7)]
    back_re = jnp.concatenate(
        [on_cos[0]] + [on_cos[c] + on_sin[c + 3] for c in range(1, RADIX)], 1
    )
    back_im = jnp.concatenate(
        [-on_sin[0]] + [on_cos[c + 3] - on_sin[c] for c in range(1, RADIX)], 1
    )
    back = jnp.concatenate([back_re, back_im], 0).astype(BF16)
    out_ref[...] = dot(order, back, 1, 1).astype(BF16)


PARAMS = pltpu.CompilerParams(vmem_limit_bytes=40 * 1024 * 1024)
VMEM = pl.BlockSpec(memory_space=pltpu.VMEM)
SMEM = pl.BlockSpec(memory_space=pltpu.SMEM)


def on_device(spectral, legendre, wave_of_slot, row_points, quad_weight, grid_factor):
    levels = spectral.shape[1]
    chans = 2 * levels
    owners = lax.axis_size("wave")
    groups = lax.axis_size("lat")
    per_owner = MS // owners
    group, own = legendre.shape
    span = own // (per_owner // 2)
    rows = groups * group
    gather = rows * legendre.dtype.itemsize < 2 * chans * 4
    me = lax.axis_index("wave")
    if gather:
        leg_all = lax.all_gather(legendre, "lat", axis=0, tiled=True)
    waves = wave_of_slot[:, None]
    mine = lax.dynamic_slice_in_dim(waves, me * per_owner, per_owner)
    coeffs = spectral.reshape(chans, own)
    fourier = pl.pallas_call(
        functools.partial(fourier_kernel, span),
        out_shape=jax.ShapeDtypeStruct((group, per_owner, chans), BF16),
        in_specs=[VMEM] * 3,
        out_specs=VMEM,
        compiler_params=PARAMS,
        name="fourier",
    )(mine, coeffs, legendre)
    arrived = lax.all_to_all(fourier, "wave", split_axis=0, concat_axis=1, tiled=True)[0]

    count = row_points[0, me]
    quarter = count // RADIX
    padded = -(-(grid_factor.shape[2] // RADIX) // CHUNK) * CHUNK
    row = jnp.pad(lax.dynamic_index_in_dim(grid_factor[0], me, 0, keepdims=False), (0, padded))
    factors = jnp.stack(
        [lax.dynamic_slice_in_dim(row, t * quarter, padded) for t in range(RADIX)]
    )
    points = count.astype(F32)
    info = jnp.stack([points, quad_weight[0, me] / points])
    back = pl.pallas_call(
        transform_kernel,
        out_shape=jax.ShapeDtypeStruct((MS, chans), BF16),
        in_specs=[SMEM] + [VMEM] * 3,
        out_specs=VMEM,
        scratch_shapes=[pltpu.VMEM((7 * levels, 2 * MS // RADIX), F32)],
        compiler_params=PARAMS,
        name="transform",
    )(info, waves, arrived, factors)
    returned = lax.all_to_all(back[None], "wave", split_axis=1, concat_axis=0, tiled=True)
    if gather:
        returned = lax.all_gather(returned, "lat", axis=0, tiled=True)
    table = leg_all if gather else legendre
    by_slot = returned.transpose(1, 0, 2).reshape(per_owner * table.shape[0], chans)
    out = pl.pallas_call(
        functools.partial(output_kernel, span),
        out_shape=jax.ShapeDtypeStruct((chans, own), F32),
        in_specs=[VMEM] * 3,
        out_specs=VMEM,
        compiler_params=PARAMS,
        name="output",
    )(mine, table, by_slot)
    if not gather:
        out = lax.psum(out, "lat")
    return out.reshape(2, levels, own)


def solution(mesh):
    return jax.shard_map(
        on_device,
        mesh=mesh,
        in_specs=(
            P(None, None, "wave"),
            P("lat", "wave"),
            P(),
            P("lat", None),
            P("lat", None),
            P("lat", None, None),
        ),
        out_specs=P(None, None, "wave"),
        check_vma=False,
    )
```

```python
import functools
import math

import jax
import jax.numpy as jnp
from jax import lax
from jax.experimental import pallas as pl
from jax.experimental.pallas import tpu as pltpu
from jax.sharding import PartitionSpec as P

TRUNC = 3999
M0 = 3488
MS = 512

F32 = jnp.float32
BF16 = jnp.bfloat16
MESH = pl.DeviceIdType.MESH
RADIX = 4
CHUNK = 512


def dot(a, b, ca, cb):
    return lax.dot_general(a, b, (((ca,), (cb,)), ((), ())), preferred_element_type=F32)


def column_bounds(waves, first_slot, span):
    slot = first_slot + lax.broadcasted_iota(jnp.int32, waves.shape, 0)
    pair = slot // 2
    length = TRUNC + 1 - waves
    low = slot % 2 == 0
    begin = jnp.where(low, pair * span, (pair + 1) * span - length)
    end = jnp.where(low, pair * span + length, (pair + 1) * span)
    return begin, end


def prepare_kernel(span, points_ref, waves_ref, spec_ref, leg_ref, grid_ref, out_ref, factor_ref, acc_ref, row_ref):
    me = lax.axis_index("wave")
    group, own = leg_ref.shape
    slots = acc_ref.shape[1]
    for first in range(0, slots, 8):
        c0 = first // 2 * span // 128 * 128
        c1 = min(-(-((first // 2 + 4) * span) // 128) * 128, own)
        waves = waves_ref[pl.ds(pl.multiple_of(me * slots + first, 8), 8), :]
        begin, end = column_bounds(waves, first, span)
        column = c0 + lax.broadcasted_iota(jnp.int32, (8, c1 - c0), 1)
        inside = (column >= begin) & (column < end)
        rows = leg_ref[:, c0:c1].astype(F32)
        masked = jnp.concatenate(
            [jnp.where(inside, rows[r : r + 1, :], 0.0) for r in range(group)], 0
        ).astype(BF16)
        sums = dot(masked, spec_ref[:, c0:c1], 1, 1)
        for r in range(group):
            acc_ref[r, first : first + 8, :] = sums[8 * r : 8 * r + 8, :]
    for r in range(group):
        out_ref[r] = acc_ref[r].T.astype(BF16)
    wide = row_ref.shape[1]
    row_ref[...] = jnp.zeros_like(row_ref)
    row_ref[:, : grid_ref.shape[1]] = grid_ref[pl.ds(me, 1), :]
    row = row_ref[...]
    quarter = points_ref[0, me] // RADIX
    for t in range(RADIX):
        shifted = pltpu.roll(row, wide - t * quarter, 1) if t else row
        factor_ref[t : t + 1, :] = shifted[:, : factor_ref.shape[1]]


def output_kernel(span, waves_ref, leg_ref, back_ref, out_ref, held_ref):
    me = lax.axis_index("wave")
    groups, group, own = leg_ref.shape
    rows, _, slots = back_ref.shape
    for r in range(rows):
        held_ref[slots * r : slots * (r + 1), :] = back_ref[r].astype(F32).T
    for c0 in range(0, own, CHUNK):
        c1 = min(c0 + CHUNK, own)
        p0, p1 = c0 // span, (c1 - 1) // span + 1
        column = c0 + lax.broadcasted_iota(jnp.int32, (1, c1 - c0), 1)
        part = jnp.concatenate([leg_ref[g, :, c0:c1].astype(F32) for g in range(groups)], 0)
        masked, left = [], []
        for pair in range(p0, p1):
            split = pair * span + TRUNC + 1 - waves_ref[me * slots + 2 * pair]
            low = (column >= pair * span) & (column < split)
            high = (column >= split) & (column < (pair + 1) * span)
            masked.append(jnp.where(low, part, 0.0))
            masked.append(jnp.where(high, part, 0.0))
            left.append(held_ref[pl.ds(2 * pair, rows, stride=slots), :])
            left.append(held_ref[pl.ds(2 * pair + 1, rows, stride=slots), :])
        right = jnp.concatenate(masked, 0).astype(BF16)
        out_ref[:, c0:c1] = dot(jnp.concatenate(left, 0).astype(BF16), right, 0, 0)


def sine_turns(v):
    y = v * v
    total = jnp.full_like(v, -((2 * math.pi) ** 11) / math.factorial(11))
    for power in (9, 7, 5, 3, 1):
        sign = 1.0 if power % 4 == 1 else -1.0
        total = total * y + sign * (2 * math.pi) ** power / math.factorial(power)
    return total * v


def angle_rows(count, start, width):
    row = lax.broadcasted_iota(jnp.int32, (32, width), 0)
    k = start + lax.broadcasted_iota(jnp.int32, (32, width), 1)
    mult = jnp.where(row < 8, M0 + 64 * row, jnp.where(row < 24, 4 * (row - 8), row - 24))
    product = (mult * k).astype(F32)
    inverse = 1.0 / count
    rest = product - count * jnp.round(product * inverse)
    turn = rest * inverse
    size = jnp.abs(turn)
    folded = jnp.minimum(size, 0.5 - size)
    return sine_turns(0.25 - size), jnp.where(turn < 0, -1.0, 1.0) * sine_turns(folded)


def halves(x):
    high = x.astype(BF16)
    return high, (x - high.astype(F32)).astype(BF16)


def order_matrix(waves):
    each = MS // RADIX
    column = lax.broadcasted_iota(jnp.int32, (MS, MS), 1)
    wave = M0 + RADIX * (column % each) + column // each
    return (waves == wave).astype(F32).astype(BF16)


def transform_kernel(
    owners, groups, points_ref, weight_ref, waves_ref, four_ref, factor_ref,
    out_ref, came_ref, leave_ref, acc_ref, high_ref, low_ref, turn_ref,
    send_four, recv_four, send_back, recv_back,
):
    me, here = lax.axis_index("wave"), lax.axis_index("lat")
    lats = lax.axis_size("lat")
    base = here * owners if groups > 1 else 0
    offsets = [(w, l) for l in range(groups) for w in range(owners) if w or l]

    def peer(offset):
        return lax.rem(me + offset[0], owners), lax.rem(here + offset[1], lats)

    barrier = pltpu.get_barrier_semaphore()
    for offset in offsets:
        pl.semaphore_signal(barrier, inc=1, device_id=peer(offset), device_id_type=MESH)
    pl.semaphore_wait(barrier, len(offsets))

    def four_copy(step, to, owner):
        return pltpu.make_async_remote_copy(
            src_ref=four_ref.at[to],
            dst_ref=came_ref.at[owner],
            send_sem=send_four.at[step],
            recv_sem=recv_four.at[owner],
            device_id=(to, here),
            device_id_type=MESH,
        )

    for step in range(1, owners):
        four_copy(step, lax.rem(me + step, owners), me).start()
    came_ref[me] = four_ref[me]

    count = points_ref[0, me].astype(F32)
    scale = weight_ref[0, me] / count
    quarter = count * 0.25
    levels = four_ref.shape[1] // 2
    each = MS // RADIX
    order = order_matrix(waves_ref[...])

    def make_tables(index, carry):
        start = index * CHUNK
        cos, sin = angle_rows(count, start, CHUNK)
        cos_b, sin_b = cos[8:24], sin[8:24]
        table = jnp.concatenate(
            [cos[a : a + 1] * cos_b - sin[a : a + 1] * sin_b for a in range(8)]
            + [sin[a : a + 1] * cos_b + cos[a : a + 1] * sin_b for a in range(8)],
            0,
        )
        high, low = halves(table)
        high_ref[index] = high
        low_ref[index] = low
        turn_ref[index, :8] = cos[24:32]
        turn_ref[index, 8:] = sin[24:32]
        return carry

    chunks = factor_ref.shape[1] // CHUNK
    lax.fori_loop(0, chunks, make_tables, 0)
    acc_ref[...] = jnp.zeros_like(acc_ref)

    for step in range(1, owners):
        four_copy(step, lax.rem(me + step, owners), me).wait_send()
        owner = lax.rem(me + owners - step, owners)
        four_copy(step, owner, owner).wait_recv()
    arrived = jnp.concatenate([came_ref[w] for w in range(owners)], 1)
    ordered = dot(arrived, order, 1, 0)
    real = [ordered[:levels, each * c : each * (c + 1)] for c in range(RADIX)]
    imag = [ordered[levels:, each * c : each * (c + 1)] for c in range(RADIX)]
    left = jnp.concatenate(
        [jnp.concatenate([real[c], -imag[c]], 1) for c in range(RADIX)]
        + [jnp.concatenate([imag[c], real[c]], 1) for c in range(1, RADIX)],
        0,
    ).astype(BF16)

    def step(index, carry):
        start = index * CHUNK
        high, low = high_ref[index], low_ref[index]
        turns = turn_ref[index]
        mixed = dot(left, high, 1, 0) + dot(left, low, 1, 0)
        h = [mixed[levels * i : levels * (i + 1)] for i in range(7)]
        c1, c2, c3 = turns[1:2], turns[2:3], turns[3:4]
        s1, s2, s3 = turns[9:10], turns[10:11], turns[11:12]
        re1, im1 = h[1] * c1 - h[4] * s1, h[1] * s1 + h[4] * c1
        re2 = h[2] * c2 - h[5] * s2
        re3, im3 = h[3] * c3 - h[6] * s3, h[3] * s3 + h[6] * c3
        e, f, p, d = h[0] + re2, h[0] - re2, re1 + re3, im1 - im3
        k = (start + lax.broadcasted_iota(jnp.int32, (1, CHUNK), 1)).astype(F32)
        g = jnp.where(k < quarter, factor_ref[:, pl.ds(pl.multiple_of(start, CHUNK), CHUNK)], 0.0)
        q0, q1, q2, q3 = g[0:1] * (e + p), g[1:2] * (f - d), g[2:3] * (e - p), g[3:4] * (f + d)
        x, y = q0 - q2, q1 - q3
        u, v = q0 + q2, q1 + q3
        w = u - v
        turned = jnp.concatenate(
            [
                u + v,
                x * c1 - y * s1,
                w * c2,
                x * c3 + y * s3,
                -(x * s1 + y * c1),
                -(w * s2),
                y * c3 - x * s3,
            ],
            0,
        )
        t_high, t_low = halves(turned)
        acc_ref[...] += dot(t_high, high, 1, 1) + dot(t_low, high, 1, 1) + dot(t_high, low, 1, 1)
        return carry

    lax.fori_loop(0, chunks, step, 0)
    total = acc_ref[...] * scale
    on_cos = [total[levels * i : levels * (i + 1), :each] for i in range(7)]
    on_sin = [total[levels * i : levels * (i + 1), each:] for i in range(7)]
    back_re = jnp.concatenate(
        [on_cos[0]] + [on_cos[c] + on_sin[c + 3] for c in range(1, RADIX)], 1
    )
    back_im = jnp.concatenate(
        [-on_sin[0]] + [on_cos[c + 3] - on_sin[c] for c in range(1, RADIX)], 1
    )
    back = jnp.concatenate([back_re, back_im], 0).astype(BF16)
    by_slot = dot(back, order, 1, 1).astype(BF16)
    slots = four_ref.shape[2]
    for w in range(owners):
        leave_ref[w] = by_slot[:, slots * w : slots * (w + 1)]

    def back_copy(step, to, row):
        return pltpu.make_async_remote_copy(
            src_ref=leave_ref.at[to[0]],
            dst_ref=out_ref.at[row],
            send_sem=send_back.at[step],
            recv_sem=recv_back.at[row],
            device_id=to,
            device_id_type=MESH,
        )

    for step, offset in enumerate(offsets):
        back_copy(step, peer(offset), base + me).start()
    out_ref[base + me] = leave_ref[me]
    for step, offset in enumerate(offsets):
        back_copy(step, peer(offset), base + me).wait_send()
        source = lax.rem(me + owners - offset[0], owners), lax.rem(here + lats - offset[1], lats)
        row = source[1] * owners + source[0] if groups > 1 else source[0]
        back_copy(step, source, row).wait_recv()


PARAMS = pltpu.CompilerParams(vmem_limit_bytes=40 * 1024 * 1024)
VMEM = pl.BlockSpec(memory_space=pltpu.VMEM)
SMEM = pl.BlockSpec(memory_space=pltpu.SMEM)


def on_device(spectral, legendre, wave_of_slot, row_points, quad_weight, grid_factor):
    levels = spectral.shape[1]
    chans = 2 * levels
    owners = lax.axis_size("wave")
    groups = lax.axis_size("lat")
    per_owner = MS // owners
    group, own = legendre.shape
    span = own // (per_owner // 2)
    gather = groups * group * legendre.dtype.itemsize < 2 * chans * 4
    table = lax.all_gather(legendre, "lat") if gather else legendre[None]
    waves = wave_of_slot[:, None]
    coeffs = spectral.reshape(chans, own)
    length = grid_factor.shape[2]
    padded = -(-(length // RADIX) // CHUNK) * CHUNK
    wide = -(-length // 128) * 128
    fourier, factors = pl.pallas_call(
        functools.partial(prepare_kernel, span),
        out_shape=[
            jax.ShapeDtypeStruct((group, chans, per_owner), BF16),
            jax.ShapeDtypeStruct((RADIX, padded), F32),
        ],
        in_specs=[SMEM] + [VMEM] * 4,
        out_specs=[VMEM] * 2,
        scratch_shapes=[pltpu.VMEM((group, per_owner, chans), F32), pltpu.VMEM((1, wide), F32)],
        compiler_params=PARAMS,
        name="prepare",
    )(row_points, waves, coeffs, legendre, grid_factor[0])
    used = groups if gather else 1
    others = owners * used - 1
    back = pl.pallas_call(
        functools.partial(transform_kernel, owners, used),
        out_shape=jax.ShapeDtypeStruct((owners * used, chans, per_owner), BF16),
        in_specs=[SMEM] * 2 + [VMEM] * 3,
        out_specs=VMEM,
        scratch_shapes=[
            pltpu.VMEM((owners, chans, per_owner), BF16),
            pltpu.VMEM((owners, chans, per_owner), BF16),
            pltpu.VMEM((7 * levels, 2 * MS // RADIX), F32),
            pltpu.VMEM((padded // CHUNK, 2 * MS // RADIX, CHUNK), BF16),
            pltpu.VMEM((padded // CHUNK, 2 * MS // RADIX, CHUNK), BF16),
            pltpu.VMEM((padded // CHUNK, 16, CHUNK), F32),
            pltpu.SemaphoreType.DMA((owners,)),
            pltpu.SemaphoreType.DMA((owners,)),
            pltpu.SemaphoreType.DMA((others,)),
            pltpu.SemaphoreType.DMA((owners * used,)),
        ],
        compiler_params=pltpu.CompilerParams(
            collective_id=0, has_side_effects=True, vmem_limit_bytes=40 * 1024 * 1024
        ),
        name="transform",
    )(row_points, quad_weight, waves, fourier, factors)
    out = pl.pallas_call(
        functools.partial(output_kernel, span),
        out_shape=jax.ShapeDtypeStruct((chans, own), F32),
        in_specs=[SMEM] + [VMEM] * 2,
        out_specs=VMEM,
        scratch_shapes=[pltpu.VMEM((owners * used * per_owner, chans), F32)],
        compiler_params=PARAMS,
        name="output",
    )(wave_of_slot, table, back)
    if not gather:
        out = lax.psum(out, "lat")
    return out.reshape(2, levels, own)


def solution(mesh):
    return jax.shard_map(
        on_device,
        mesh=mesh,
        in_specs=(
            P(None, None, "wave"),
            P("lat", "wave"),
            P(),
            P("lat", None),
            P("lat", None),
            P("lat", None, None),
        ),
        out_specs=P(None, None, "wave"),
        check_vma=False,
    )
```

```python
import functools
import math

import jax
import jax.numpy as jnp
from jax import lax
from jax.experimental import pallas as pl
from jax.experimental.pallas import tpu as pltpu
from jax.sharding import PartitionSpec as P

TRUNC = 3999
M0 = 3488
MS = 512

F32 = jnp.float32
BF16 = jnp.bfloat16
MESH = pl.DeviceIdType.MESH
RADIX = 4
CHUNK = 512


def dot(a, b, ca, cb):
    return lax.dot_general(a, b, (((ca,), (cb,)), ((), ())), preferred_element_type=F32)


def column_bounds(waves, first_slot, span):
    slot = first_slot + lax.broadcasted_iota(jnp.int32, waves.shape, 0)
    pair = slot // 2
    length = TRUNC + 1 - waves
    low = slot % 2 == 0
    begin = jnp.where(low, pair * span, (pair + 1) * span - length)
    end = jnp.where(low, pair * span + length, (pair + 1) * span)
    return begin, end


def wave_column(waves_ref):
    row = waves_ref[...].astype(F32)
    return jnp.broadcast_to(row, (8, row.shape[1])).T[:, :1]


def prepare_kernel(
    span, points_ref, waves_ref, spec_hbm, leg_hbm, grid_hbm, out_ref, factor_ref, packed_ref,
    acc_ref, row_ref, column_ref, pack_ref, spec_ref, leg_ref, grid_ref, sems,
):
    me = lax.axis_index("wave")
    copies = [
        pltpu.make_async_copy(source, target, sems.at[i])
        for i, (source, target) in enumerate(
            ((spec_hbm, spec_ref), (leg_hbm, leg_ref), (grid_hbm, grid_ref))
        )
    ]
    for copy in copies:
        copy.start()
    column_ref[...] = wave_column(waves_ref).astype(jnp.int32)
    for copy in copies:
        copy.wait()
    group, own = leg_ref.shape
    length = packed_ref.shape[1]
    for piece in range(packed_ref.shape[0] // group):
        first, last = piece * length, min((piece + 1) * length, own)
        if last - first < length:
            pack_ref[group * piece : group * (piece + 1), :] = jnp.zeros((group, length), F32)
        pack_ref[group * piece : group * (piece + 1), : last - first] = leg_ref[
            :, first:last
        ].astype(F32)
    packed_ref[...] = pack_ref[...].astype(BF16)
    slots = acc_ref.shape[1]
    for first in range(0, slots, 8):
        c0 = first // 2 * span // 128 * 128
        c1 = min(-(-((first // 2 + 4) * span) // 128) * 128, own)
        waves = column_ref[pl.ds(pl.multiple_of(me * slots + first, 8), 8), :]
        begin, end = column_bounds(waves, first, span)
        column = c0 + lax.broadcasted_iota(jnp.int32, (8, c1 - c0), 1)
        inside = (column >= begin) & (column < end)
        rows = leg_ref[:, c0:c1].astype(F32)
        masked = jnp.concatenate(
            [jnp.where(inside, rows[r : r + 1, :], 0.0) for r in range(group)], 0
        ).astype(BF16)
        sums = dot(masked, spec_ref[:, c0:c1], 1, 1)
        for r in range(group):
            acc_ref[r, first : first + 8, :] = sums[8 * r : 8 * r + 8, :]
    for r in range(group):
        out_ref[r] = acc_ref[r].T.astype(BF16)
    wide = row_ref.shape[1]
    row_ref[...] = jnp.zeros_like(row_ref)
    row_ref[:, : grid_ref.shape[1]] = grid_ref[pl.ds(me, 1), :]
    row = row_ref[...]
    quarter = points_ref[0, me] // RADIX
    for t in range(RADIX):
        shifted = pltpu.roll(row, wide - t * quarter, 1) if t else row
        factor_ref[t : t + 1, :] = shifted[:, : factor_ref.shape[1]]


def output_kernel(span, group, waves_ref, leg_ref, back_ref, out_ref, held_ref):
    me = lax.axis_index("wave")
    groups, packed, length = leg_ref.shape
    own = out_ref.shape[1]
    rows, _, slots = back_ref.shape
    for r in range(rows):
        held_ref[slots * r : slots * (r + 1), :] = back_ref[r].astype(F32).T
    for at in range(0, length, CHUNK):
        parts = [leg_ref[g, :, at : min(at + CHUNK, length)].astype(F32) for g in range(groups)]
        for piece in range(packed // group):
            c0 = piece * length + at
            c1 = min(c0 + CHUNK, (piece + 1) * length, own)
            if c1 <= c0:
                continue
            p0, p1 = c0 // span, (c1 - 1) // span + 1
            column = c0 + lax.broadcasted_iota(jnp.int32, (1, c1 - c0), 1)
            part = jnp.concatenate(
                [p[group * piece : group * (piece + 1), : c1 - c0] for p in parts], 0
            )
            masked, left = [], []
            for pair in range(p0, p1):
                split = pair * span + TRUNC + 1 - waves_ref[me * slots + 2 * pair]
                low = (column >= pair * span) & (column < split)
                high = (column >= split) & (column < (pair + 1) * span)
                masked.append(jnp.where(low, part, 0.0))
                masked.append(jnp.where(high, part, 0.0))
                left.append(held_ref[pl.ds(2 * pair, rows, stride=slots), :])
                left.append(held_ref[pl.ds(2 * pair + 1, rows, stride=slots), :])
            right = jnp.concatenate(masked, 0).astype(BF16)
            out_ref[:, c0:c1] = dot(jnp.concatenate(left, 0).astype(BF16), right, 0, 0)


def sine_turns(v):
    y = v * v
    total = jnp.full_like(v, -((2 * math.pi) ** 11) / math.factorial(11))
    for power in (9, 7, 5, 3, 1):
        sign = 1.0 if power % 4 == 1 else -1.0
        total = total * y + sign * (2 * math.pi) ** power / math.factorial(power)
    return total * v


def angle_rows(count, start, width):
    row = lax.broadcasted_iota(jnp.int32, (32, width), 0)
    k = start + lax.broadcasted_iota(jnp.int32, (32, width), 1)
    mult = jnp.where(row < 8, M0 + 64 * row, jnp.where(row < 24, 4 * (row - 8), row - 24))
    product = (mult * k).astype(F32)
    inverse = 1.0 / count
    rest = product - count * jnp.round(product * inverse)
    turn = rest * inverse
    size = jnp.abs(turn)
    folded = jnp.minimum(size, 0.5 - size)
    return sine_turns(0.25 - size), jnp.where(turn < 0, -1.0, 1.0) * sine_turns(folded)


def halves(x):
    high = x.astype(BF16)
    return high, (x - high.astype(F32)).astype(BF16)


def order_matrix(waves):
    each = MS // RADIX
    column = lax.broadcasted_iota(jnp.int32, (MS, MS), 1)
    wave = M0 + RADIX * (column % each) + column // each
    return (waves == wave.astype(F32)).astype(F32).astype(BF16)


def transform_kernel(
    owners, groups, points_ref, weight_ref, waves_ref, four_ref, factor_ref, leg_ref,
    out_ref, table_ref, came_ref, leave_ref, acc_ref, high_ref, low_ref, turn_ref,
    send_four, recv_four, send_back, recv_back, send_leg, recv_leg,
):
    me, here = lax.axis_index("wave"), lax.axis_index("lat")
    lats = lax.axis_size("lat")
    base = here * owners if groups > 1 else 0
    offsets = [(w, l) for l in range(groups) for w in range(owners) if w or l]

    def peer(offset):
        return lax.rem(me + offset[0], owners), lax.rem(here + offset[1], lats)

    barrier = pltpu.get_barrier_semaphore()
    for offset in offsets:
        pl.semaphore_signal(barrier, inc=1, device_id=peer(offset), device_id_type=MESH)
    pl.semaphore_wait(barrier, len(offsets))

    def four_copy(step, to, owner):
        return pltpu.make_async_remote_copy(
            src_ref=four_ref.at[to],
            dst_ref=came_ref.at[owner],
            send_sem=send_four.at[step],
            recv_sem=recv_four.at[owner],
            device_id=(to, here),
            device_id_type=MESH,
        )

    for step in range(1, owners):
        four_copy(step, lax.rem(me + step, owners), me).start()
    came_ref[me] = four_ref[me]

    sibling = here + 1 - 2 * lax.rem(here, 2)

    def leg_copy(at, source, row, to):
        return pltpu.make_async_remote_copy(
            src_ref=source,
            dst_ref=table_ref.at[row],
            send_sem=send_leg.at[at],
            recv_sem=recv_leg.at[row],
            device_id=(me, to),
            device_id_type=MESH,
        )

    if groups > 1:
        for step in range(2, groups, 2):
            leg_copy(step, leg_ref, here, lax.rem(here + step, lats)).start()
        leg_copy(0, leg_ref, here, sibling).start()
    table_ref[here if groups > 1 else 0] = leg_ref[...]

    count = points_ref[0, me].astype(F32)
    scale = weight_ref[0, me] / count
    quarter = count * 0.25
    levels = four_ref.shape[1] // 2
    each = MS // RADIX
    order = order_matrix(wave_column(waves_ref))

    def make_tables(index, carry):
        start = index * CHUNK
        cos, sin = angle_rows(count, start, CHUNK)
        cos_b, sin_b = cos[8:24], sin[8:24]
        table = jnp.concatenate(
            [cos[a : a + 1] * cos_b - sin[a : a + 1] * sin_b for a in range(8)]
            + [sin[a : a + 1] * cos_b + cos[a : a + 1] * sin_b for a in range(8)],
            0,
        )
        high, low = halves(table)
        high_ref[index] = high
        low_ref[index] = low
        turn_ref[index, :8] = cos[24:32]
        turn_ref[index, 8:] = sin[24:32]
        return carry

    chunks = factor_ref.shape[1] // CHUNK
    lax.fori_loop(0, chunks, make_tables, 0)
    acc_ref[...] = jnp.zeros_like(acc_ref)

    for step in range(1, owners):
        four_copy(step, lax.rem(me + step, owners), me).wait_send()
        owner = lax.rem(me + owners - step, owners)
        four_copy(step, owner, owner).wait_recv()
    arrived = jnp.concatenate([came_ref[w] for w in range(owners)], 1)
    ordered = dot(arrived, order, 1, 0)
    real = [ordered[:levels, each * c : each * (c + 1)] for c in range(RADIX)]
    imag = [ordered[levels:, each * c : each * (c + 1)] for c in range(RADIX)]
    left = jnp.concatenate(
        [jnp.concatenate([real[c], -imag[c]], 1) for c in range(RADIX)]
        + [jnp.concatenate([imag[c], real[c]], 1) for c in range(1, RADIX)],
        0,
    ).astype(BF16)

    def step(index, carry):
        start = index * CHUNK
        high, low = high_ref[index], low_ref[index]
        turns = turn_ref[index]
        mixed = dot(left, high, 1, 0) + dot(left, low, 1, 0)
        h = [mixed[levels * i : levels * (i + 1)] for i in range(7)]
        c1, c2, c3 = turns[1:2], turns[2:3], turns[3:4]
        s1, s2, s3 = turns[9:10], turns[10:11], turns[11:12]
        re1, im1 = h[1] * c1 - h[4] * s1, h[1] * s1 + h[4] * c1
        re2 = h[2] * c2 - h[5] * s2
        re3, im3 = h[3] * c3 - h[6] * s3, h[3] * s3 + h[6] * c3
        e, f, p, d = h[0] + re2, h[0] - re2, re1 + re3, im1 - im3
        k = (start + lax.broadcasted_iota(jnp.int32, (1, CHUNK), 1)).astype(F32)
        g = jnp.where(k < quarter, factor_ref[:, pl.ds(pl.multiple_of(start, CHUNK), CHUNK)], 0.0)
        q0, q1, q2, q3 = g[0:1] * (e + p), g[1:2] * (f - d), g[2:3] * (e - p), g[3:4] * (f + d)
        x, y = q0 - q2, q1 - q3
        u, v = q0 + q2, q1 + q3
        w = u - v
        turned = jnp.concatenate(
            [
                u + v,
                x * c1 - y * s1,
                w * c2,
                x * c3 + y * s3,
                -(x * s1 + y * c1),
                -(w * s2),
                y * c3 - x * s3,
            ],
            0,
        )
        t_high, t_low = halves(turned)
        acc_ref[...] += dot(t_high, high, 1, 1) + dot(t_low, high, 1, 1) + dot(t_high, low, 1, 1)
        return carry

    lax.fori_loop(0, chunks, step, 0)
    total = acc_ref[...] * scale
    on_cos = [total[levels * i : levels * (i + 1), :each] for i in range(7)]
    on_sin = [total[levels * i : levels * (i + 1), each:] for i in range(7)]
    back_re = jnp.concatenate(
        [on_cos[0]] + [on_cos[c] + on_sin[c + 3] for c in range(1, RADIX)], 1
    )
    back_im = jnp.concatenate(
        [-on_sin[0]] + [on_cos[c + 3] - on_sin[c] for c in range(1, RADIX)], 1
    )
    back = jnp.concatenate([back_re, back_im], 0).astype(BF16)
    by_slot = dot(back, order, 1, 1).astype(BF16)
    slots = four_ref.shape[2]
    for w in range(owners):
        leave_ref[w] = by_slot[:, slots * w : slots * (w + 1)]

    def back_copy(step, to, row):
        return pltpu.make_async_remote_copy(
            src_ref=leave_ref.at[to[0]],
            dst_ref=out_ref.at[row],
            send_sem=send_back.at[step],
            recv_sem=recv_back.at[row],
            device_id=to,
            device_id_type=MESH,
        )

    for step, offset in enumerate(offsets):
        back_copy(step, peer(offset), base + me).start()
    out_ref[base + me] = leave_ref[me]
    if groups > 1:
        for step in range(2, groups, 2):
            row = lax.rem(here + lats - step, lats)
            leg_copy(step, leg_ref, row, row).wait_recv()
            leg_copy(step + 1, table_ref.at[row], row, sibling).start()
        for step in range(0, groups, 2):
            leg_copy(step, leg_ref, here, sibling).wait_send()
            row = lax.rem(sibling + lats - step, lats)
            leg_copy(step, leg_ref, row, sibling).wait_recv()
        for step in range(2, groups, 2):
            row = lax.rem(here + lats - step, lats)
            leg_copy(step + 1, table_ref.at[row], row, sibling).wait_send()
    for step, offset in enumerate(offsets):
        back_copy(step, peer(offset), base + me).wait_send()
        source = lax.rem(me + owners - offset[0], owners), lax.rem(here + lats - offset[1], lats)
        row = source[1] * owners + source[0] if groups > 1 else source[0]
        back_copy(step, source, row).wait_recv()


PARAMS = pltpu.CompilerParams(vmem_limit_bytes=40 * 1024 * 1024)
VMEM = pl.BlockSpec(memory_space=pltpu.VMEM)
HBM = pl.BlockSpec(memory_space=pltpu.HBM)
SMEM = pl.BlockSpec(memory_space=pltpu.SMEM)


def on_device(spectral, legendre, wave_of_slot, row_points, quad_weight, grid_factor):
    levels = spectral.shape[1]
    chans = 2 * levels
    owners = lax.axis_size("wave")
    groups = lax.axis_size("lat")
    per_owner = MS // owners
    group, own = legendre.shape
    span = own // (per_owner // 2)
    gather = groups % 2 == 0 and groups * group * legendre.dtype.itemsize < 2 * chans * 4
    pieces = max(1, 16 // group)
    packed = -(-own // (pieces * 128)) * 128
    waves = wave_of_slot[None]
    coeffs = spectral.reshape(chans, own)
    length = grid_factor.shape[2]
    padded = -(-(length // RADIX) // CHUNK) * CHUNK
    wide = -(-length // 128) * 128
    fourier, factors, mine = pl.pallas_call(
        functools.partial(prepare_kernel, span),
        out_shape=[
            jax.ShapeDtypeStruct((group, chans, per_owner), BF16),
            jax.ShapeDtypeStruct((RADIX, padded), F32),
            jax.ShapeDtypeStruct((pieces * group, packed), BF16),
        ],
        in_specs=[SMEM, VMEM] + [HBM] * 3,
        out_specs=[VMEM] * 3,
        scratch_shapes=[
            pltpu.VMEM((group, per_owner, chans), F32),
            pltpu.VMEM((1, wide), F32),
            pltpu.VMEM((MS, 1), jnp.int32),
            pltpu.VMEM((pieces * group, packed), F32),
            pltpu.VMEM((chans, own), BF16),
            pltpu.VMEM((group, own), BF16),
            pltpu.VMEM(grid_factor.shape[1:], F32),
            pltpu.SemaphoreType.DMA((3,)),
        ],
        compiler_params=pltpu.CompilerParams(vmem_limit_bytes=62 * 1024 * 1024),
        name="prepare",
    )(row_points, waves, coeffs, legendre, grid_factor[0])
    used = groups if gather else 1
    others = owners * used - 1
    back, table = pl.pallas_call(
        functools.partial(transform_kernel, owners, used),
        out_shape=[
            jax.ShapeDtypeStruct((owners * used, chans, per_owner), BF16),
            jax.ShapeDtypeStruct((used, pieces * group, packed), BF16),
        ],
        in_specs=[SMEM] * 2 + [VMEM] * 4,
        out_specs=[VMEM] * 2,
        scratch_shapes=[
            pltpu.VMEM((owners, chans, per_owner), BF16),
            pltpu.VMEM((owners, chans, per_owner), BF16),
            pltpu.VMEM((7 * levels, 2 * MS // RADIX), F32),
            pltpu.VMEM((padded // CHUNK, 2 * MS // RADIX, CHUNK), BF16),
            pltpu.VMEM((padded // CHUNK, 2 * MS // RADIX, CHUNK), BF16),
            pltpu.VMEM((padded // CHUNK, 16, CHUNK), F32),
            pltpu.SemaphoreType.DMA((owners,)),
            pltpu.SemaphoreType.DMA((owners,)),
            pltpu.SemaphoreType.DMA((others,)),
            pltpu.SemaphoreType.DMA((owners * used,)),
            pltpu.SemaphoreType.DMA((max(used, 2),)),
            pltpu.SemaphoreType.DMA((used,)),
        ],
        compiler_params=pltpu.CompilerParams(
            collective_id=0, has_side_effects=True, vmem_limit_bytes=40 * 1024 * 1024
        ),
        name="transform",
    )(row_points, quad_weight, waves, fourier, factors, mine)
    out = pl.pallas_call(
        functools.partial(output_kernel, span, group),
        out_shape=jax.ShapeDtypeStruct((chans, own), F32),
        in_specs=[SMEM] + [VMEM] * 2,
        out_specs=VMEM,
        scratch_shapes=[pltpu.VMEM((owners * used * per_owner, chans), F32)],
        compiler_params=PARAMS,
        name="output",
    )(wave_of_slot, table, back)
    if not gather:
        out = lax.psum(out, "lat")
    return out.reshape(2, levels, own)


def solution(mesh):
    return jax.shard_map(
        on_device,
        mesh=mesh,
        in_specs=(
            P(None, None, "wave"),
            P("lat", "wave"),
            P(),
            P("lat", None),
            P("lat", None),
            P("lat", None, None),
        ),
        out_specs=P(None, None, "wave"),
        check_vma=False,
    )
```

```python
import functools
import math

import jax
import jax.numpy as jnp
from jax import lax
from jax.experimental import pallas as pl
from jax.experimental.pallas import tpu as pltpu
from jax.sharding import PartitionSpec as P

TRUNC = 3999
M0 = 3488
MS = 512

F32 = jnp.float32
BF16 = jnp.bfloat16
MESH = pl.DeviceIdType.MESH
RADIX = 4
CHUNK = 512


def dot(a, b, ca, cb):
    return lax.dot_general(a, b, (((ca,), (cb,)), ((), ())), preferred_element_type=F32)


def column_bounds(waves, first_slot, span):
    slot = first_slot + lax.broadcasted_iota(jnp.int32, waves.shape, 0)
    pair = slot // 2
    length = TRUNC + 1 - waves
    low = slot % 2 == 0
    begin = jnp.where(low, pair * span, (pair + 1) * span - length)
    end = jnp.where(low, pair * span + length, (pair + 1) * span)
    return begin, end


def wave_column(waves_ref):
    row = waves_ref[...].astype(F32)
    return jnp.broadcast_to(row, (8, row.shape[1])).T[:, :1]


def pack_rows(leg_ref, pack_ref, packed_ref):
    group, own = leg_ref.shape
    length = packed_ref.shape[1]
    for piece in range(packed_ref.shape[0] // group):
        first, last = piece * length, min((piece + 1) * length, own)
        if last - first < length:
            pack_ref[group * piece : group * (piece + 1), :] = jnp.zeros((group, length), F32)
        pack_ref[group * piece : group * (piece + 1), : last - first] = leg_ref[
            :, first:last
        ].astype(F32)
    packed_ref[...] = pack_ref[...].astype(BF16)


def make_fourier(span, me, column_ref, spec_ref, leg_ref, acc_ref, out_ref):
    group, own = leg_ref.shape
    slots = acc_ref.shape[1]
    for first in range(0, slots, 8):
        c0 = first // 2 * span // 128 * 128
        c1 = min(-(-((first // 2 + 4) * span) // 128) * 128, own)
        waves = column_ref[pl.ds(pl.multiple_of(me * slots + first, 8), 8), :]
        begin, end = column_bounds(waves, first, span)
        column = c0 + lax.broadcasted_iota(jnp.int32, (8, c1 - c0), 1)
        inside = (column >= begin) & (column < end)
        rows = leg_ref[:, c0:c1].astype(F32)
        masked = jnp.concatenate(
            [jnp.where(inside, rows[r : r + 1, :], 0.0) for r in range(group)], 0
        ).astype(BF16)
        sums = dot(masked, spec_ref[:, c0:c1], 1, 1)
        for r in range(group):
            acc_ref[r, first : first + 8, :] = sums[8 * r : 8 * r + 8, :]
    for r in range(group):
        out_ref[r] = acc_ref[r].T.astype(BF16)


def shift_factors(quarter, row_ref, factor_ref):
    wide = row_ref.shape[1]
    row = row_ref[...]
    for t in range(RADIX):
        shifted = pltpu.roll(row, wide - t * quarter, 1) if t else row
        factor_ref[t : t + 1, :] = shifted[:, : factor_ref.shape[1]]


def output_kernel(span, group, waves_ref, leg_ref, back_ref, out_ref, held_ref):
    me = lax.axis_index("wave")
    groups, packed, length = leg_ref.shape
    own = out_ref.shape[1]
    rows, _, slots = back_ref.shape
    for r in range(rows):
        held_ref[slots * r : slots * (r + 1), :] = back_ref[r].astype(F32).T
    for at in range(0, length, CHUNK):
        parts = [leg_ref[g, :, at : min(at + CHUNK, length)].astype(F32) for g in range(groups)]
        for piece in range(packed // group):
            c0 = piece * length + at
            c1 = min(c0 + CHUNK, (piece + 1) * length, own)
            if c1 <= c0:
                continue
            p0, p1 = c0 // span, (c1 - 1) // span + 1
            column = c0 + lax.broadcasted_iota(jnp.int32, (1, c1 - c0), 1)
            part = jnp.concatenate(
                [p[group * piece : group * (piece + 1), : c1 - c0] for p in parts], 0
            )
            masked, left = [], []
            for pair in range(p0, p1):
                split = pair * span + TRUNC + 1 - waves_ref[me * slots + 2 * pair]
                low = (column >= pair * span) & (column < split)
                high = (column >= split) & (column < (pair + 1) * span)
                masked.append(jnp.where(low, part, 0.0))
                masked.append(jnp.where(high, part, 0.0))
                left.append(held_ref[pl.ds(2 * pair, rows, stride=slots), :])
                left.append(held_ref[pl.ds(2 * pair + 1, rows, stride=slots), :])
            right = jnp.concatenate(masked, 0).astype(BF16)
            out_ref[:, c0:c1] = dot(jnp.concatenate(left, 0).astype(BF16), right, 0, 0)


def sine_turns(v):
    y = v * v
    total = jnp.full_like(v, -((2 * math.pi) ** 11) / math.factorial(11))
    for power in (9, 7, 5, 3, 1):
        sign = 1.0 if power % 4 == 1 else -1.0
        total = total * y + sign * (2 * math.pi) ** power / math.factorial(power)
    return total * v


def angle_rows(count, start, width):
    row = lax.broadcasted_iota(jnp.int32, (32, width), 0)
    k = start + lax.broadcasted_iota(jnp.int32, (32, width), 1)
    mult = jnp.where(row < 8, M0 + 64 * row, jnp.where(row < 24, 4 * (row - 8), row - 24))
    product = (mult * k).astype(F32)
    inverse = 1.0 / count
    rest = product - count * jnp.round(product * inverse)
    turn = rest * inverse
    size = jnp.abs(turn)
    folded = jnp.minimum(size, 0.5 - size)
    return sine_turns(0.25 - size), jnp.where(turn < 0, -1.0, 1.0) * sine_turns(folded)


def halves(x):
    high = x.astype(BF16)
    return high, (x - high.astype(F32)).astype(BF16)


def order_matrix(waves):
    each = MS // RADIX
    column = lax.broadcasted_iota(jnp.int32, (MS, MS), 1)
    wave = M0 + RADIX * (column % each) + column // each
    return (waves == wave.astype(F32)).astype(F32).astype(BF16)


def transform_kernel(
    span, owners, groups, points_ref, weight_ref, waves_ref, spec_hbm, rows_hbm, grid_hbm,
    out_ref, table_ref, four_ref, factor_ref, leg_ref,
    sums_ref, row_ref, column_ref, pack_ref, spec_ref, rows_ref, grid_ref, sems, came_ref, leave_ref, acc_ref, high_ref, low_ref, turn_ref,
    send_four, recv_four, send_back, recv_back, send_leg, recv_leg,
):
    me, here = lax.axis_index("wave"), lax.axis_index("lat")
    lats = lax.axis_size("lat")
    base = here * owners if groups > 1 else 0
    offsets = [(w, l) for l in range(groups) for w in range(owners) if w or l]

    def peer(offset):
        return lax.rem(me + offset[0], owners), lax.rem(here + offset[1], lats)

    loads = [
        pltpu.make_async_copy(source, target, sems.at[i])
        for i, (source, target) in enumerate(
            ((rows_hbm, rows_ref), (spec_hbm, spec_ref), (grid_hbm, grid_ref))
        )
    ]
    for load in loads:
        load.start()
    barrier = pltpu.get_barrier_semaphore()
    for offset in offsets:
        pl.semaphore_signal(barrier, inc=1, device_id=peer(offset), device_id_type=MESH)
    column_ref[...] = wave_column(waves_ref).astype(jnp.int32)
    loads[0].wait()
    pack_rows(rows_ref, pack_ref, leg_ref)
    pl.semaphore_wait(barrier, len(offsets))

    def four_copy(step, to, owner):
        return pltpu.make_async_remote_copy(
            src_ref=four_ref.at[to],
            dst_ref=came_ref.at[owner],
            send_sem=send_four.at[step],
            recv_sem=recv_four.at[owner],
            device_id=(to, here),
            device_id_type=MESH,
        )

    sibling = here + 1 - 2 * lax.rem(here, 2)

    def leg_copy(at, source, row, to):
        return pltpu.make_async_remote_copy(
            src_ref=source,
            dst_ref=table_ref.at[row],
            send_sem=send_leg.at[at],
            recv_sem=recv_leg.at[row],
            device_id=(me, to),
            device_id_type=MESH,
        )

    if groups > 1:
        for step in range(2, groups, 2):
            leg_copy(step, leg_ref, here, lax.rem(here + step, lats)).start()
        leg_copy(0, leg_ref, here, sibling).start()
    loads[1].wait()
    make_fourier(span, me, column_ref, spec_ref, rows_ref, sums_ref, four_ref)
    for step in range(1, owners):
        four_copy(step, lax.rem(me + step, owners), me).start()
    came_ref[me] = four_ref[me]
    table_ref[here if groups > 1 else 0] = leg_ref[...]
    loads[2].wait()
    row_ref[...] = jnp.zeros_like(row_ref)
    row_ref[:, : grid_ref.shape[1]] = grid_ref[pl.ds(me, 1), :]
    shift_factors(points_ref[0, me] // RADIX, row_ref, factor_ref)

    count = points_ref[0, me].astype(F32)
    scale = weight_ref[0, me] / count
    quarter = count * 0.25
    levels = four_ref.shape[1] // 2
    each = MS // RADIX
    order = order_matrix(wave_column(waves_ref))

    def make_tables(index, carry):
        start = index * CHUNK
        cos, sin = angle_rows(count, start, CHUNK)
        cos_b, sin_b = cos[8:24], sin[8:24]
        table = jnp.concatenate(
            [cos[a : a + 1] * cos_b - sin[a : a + 1] * sin_b for a in range(8)]
            + [sin[a : a + 1] * cos_b + cos[a : a + 1] * sin_b for a in range(8)],
            0,
        )
        high, low = halves(table)
        high_ref[index] = high
        low_ref[index] = low
        turn_ref[index, :8] = cos[24:32]
        turn_ref[index, 8:] = sin[24:32]
        return carry

    chunks = factor_ref.shape[1] // CHUNK
    lax.fori_loop(0, chunks, make_tables, 0)
    acc_ref[...] = jnp.zeros_like(acc_ref)

    for step in range(1, owners):
        four_copy(step, lax.rem(me + step, owners), me).wait_send()
        owner = lax.rem(me + owners - step, owners)
        four_copy(step, owner, owner).wait_recv()
    arrived = jnp.concatenate([came_ref[w] for w in range(owners)], 1)
    ordered = dot(arrived, order, 1, 0)
    real = [ordered[:levels, each * c : each * (c + 1)] for c in range(RADIX)]
    imag = [ordered[levels:, each * c : each * (c + 1)] for c in range(RADIX)]
    left = jnp.concatenate(
        [jnp.concatenate([real[c], -imag[c]], 1) for c in range(RADIX)]
        + [jnp.concatenate([imag[c], real[c]], 1) for c in range(1, RADIX)],
        0,
    ).astype(BF16)

    def step(index, carry):
        start = index * CHUNK
        high, low = high_ref[index], low_ref[index]
        turns = turn_ref[index]
        mixed = dot(left, high, 1, 0) + dot(left, low, 1, 0)
        h = [mixed[levels * i : levels * (i + 1)] for i in range(7)]
        c1, c2, c3 = turns[1:2], turns[2:3], turns[3:4]
        s1, s2, s3 = turns[9:10], turns[10:11], turns[11:12]
        re1, im1 = h[1] * c1 - h[4] * s1, h[1] * s1 + h[4] * c1
        re2 = h[2] * c2 - h[5] * s2
        re3, im3 = h[3] * c3 - h[6] * s3, h[3] * s3 + h[6] * c3
        e, f, p, d = h[0] + re2, h[0] - re2, re1 + re3, im1 - im3
        k = (start + lax.broadcasted_iota(jnp.int32, (1, CHUNK), 1)).astype(F32)
        g = jnp.where(k < quarter, factor_ref[:, pl.ds(pl.multiple_of(start, CHUNK), CHUNK)], 0.0)
        q0, q1, q2, q3 = g[0:1] * (e + p), g[1:2] * (f - d), g[2:3] * (e - p), g[3:4] * (f + d)
        x, y = q0 - q2, q1 - q3
        u, v = q0 + q2, q1 + q3
        w = u - v
        turned = jnp.concatenate(
            [
                u + v,
                x * c1 - y * s1,
                w * c2,
                x * c3 + y * s3,
                -(x * s1 + y * c1),
                -(w * s2),
                y * c3 - x * s3,
            ],
            0,
        )
        t_high, t_low = halves(turned)
        acc_ref[...] += dot(t_high, high, 1, 1) + dot(t_low, high, 1, 1) + dot(t_high, low, 1, 1)
        return carry

    lax.fori_loop(0, chunks, step, 0)
    total = acc_ref[...] * scale
    on_cos = [total[levels * i : levels * (i + 1), :each] for i in range(7)]
    on_sin = [total[levels * i : levels * (i + 1), each:] for i in range(7)]
    back_re = jnp.concatenate(
        [on_cos[0]] + [on_cos[c] + on_sin[c + 3] for c in range(1, RADIX)], 1
    )
    back_im = jnp.concatenate(
        [-on_sin[0]] + [on_cos[c + 3] - on_sin[c] for c in range(1, RADIX)], 1
    )
    back = jnp.concatenate([back_re, back_im], 0).astype(BF16)
    by_slot = dot(back, order, 1, 1).astype(BF16)
    slots = four_ref.shape[2]
    for w in range(owners):
        leave_ref[w] = by_slot[:, slots * w : slots * (w + 1)]

    def back_copy(step, to, row):
        return pltpu.make_async_remote_copy(
            src_ref=leave_ref.at[to[0]],
            dst_ref=out_ref.at[row],
            send_sem=send_back.at[step],
            recv_sem=recv_back.at[row],
            device_id=to,
            device_id_type=MESH,
        )

    for step, offset in enumerate(offsets):
        back_copy(step, peer(offset), base + me).start()
    out_ref[base + me] = leave_ref[me]
    if groups > 1:
        for step in range(2, groups, 2):
            row = lax.rem(here + lats - step, lats)
            leg_copy(step, leg_ref, row, row).wait_recv()
            leg_copy(step + 1, table_ref.at[row], row, sibling).start()
        for step in range(0, groups, 2):
            leg_copy(step, leg_ref, here, sibling).wait_send()
            row = lax.rem(sibling + lats - step, lats)
            leg_copy(step, leg_ref, row, sibling).wait_recv()
        for step in range(2, groups, 2):
            row = lax.rem(here + lats - step, lats)
            leg_copy(step + 1, table_ref.at[row], row, sibling).wait_send()
    for step, offset in enumerate(offsets):
        back_copy(step, peer(offset), base + me).wait_send()
        source = lax.rem(me + owners - offset[0], owners), lax.rem(here + lats - offset[1], lats)
        row = source[1] * owners + source[0] if groups > 1 else source[0]
        back_copy(step, source, row).wait_recv()


PARAMS = pltpu.CompilerParams(vmem_limit_bytes=40 * 1024 * 1024)
VMEM = pl.BlockSpec(memory_space=pltpu.VMEM)
HBM = pl.BlockSpec(memory_space=pltpu.HBM)
SMEM = pl.BlockSpec(memory_space=pltpu.SMEM)


def on_device(spectral, legendre, wave_of_slot, row_points, quad_weight, grid_factor):
    levels = spectral.shape[1]
    chans = 2 * levels
    owners = lax.axis_size("wave")
    groups = lax.axis_size("lat")
    per_owner = MS // owners
    group, own = legendre.shape
    span = own // (per_owner // 2)
    gather = groups % 2 == 0 and groups * group * legendre.dtype.itemsize < 2 * chans * 4
    pieces = max(1, 16 // group)
    packed = -(-own // (pieces * 128)) * 128
    waves = wave_of_slot[None]
    coeffs = spectral.reshape(chans, own)
    length = grid_factor.shape[2]
    padded = -(-(length // RADIX) // CHUNK) * CHUNK
    wide = -(-length // 128) * 128
    used = groups if gather else 1
    others = owners * used - 1
    back, table = pl.pallas_call(
        functools.partial(transform_kernel, span, owners, used),
        out_shape=[
            jax.ShapeDtypeStruct((owners * used, chans, per_owner), BF16),
            jax.ShapeDtypeStruct((used, pieces * group, packed), BF16),
        ],
        in_specs=[SMEM] * 2 + [VMEM] + [HBM] * 3,
        out_specs=[VMEM] * 2,
        scratch_shapes=[
            pltpu.VMEM((group, chans, per_owner), BF16),
            pltpu.VMEM((RADIX, padded), F32),
            pltpu.VMEM((pieces * group, packed), BF16),
            pltpu.VMEM((group, per_owner, chans), F32),
            pltpu.VMEM((1, wide), F32),
            pltpu.VMEM((MS, 1), jnp.int32),
            pltpu.VMEM((pieces * group, packed), F32),
            pltpu.VMEM((chans, own), BF16),
            pltpu.VMEM((group, own), BF16),
            pltpu.VMEM(grid_factor.shape[1:], F32),
            pltpu.SemaphoreType.DMA((3,)),
            pltpu.VMEM((owners, chans, per_owner), BF16),
            pltpu.VMEM((owners, chans, per_owner), BF16),
            pltpu.VMEM((7 * levels, 2 * MS // RADIX), F32),
            pltpu.VMEM((padded // CHUNK, 2 * MS // RADIX, CHUNK), BF16),
            pltpu.VMEM((padded // CHUNK, 2 * MS // RADIX, CHUNK), BF16),
            pltpu.VMEM((padded // CHUNK, 16, CHUNK), F32),
            pltpu.SemaphoreType.DMA((owners,)),
            pltpu.SemaphoreType.DMA((owners,)),
            pltpu.SemaphoreType.DMA((others,)),
            pltpu.SemaphoreType.DMA((owners * used,)),
            pltpu.SemaphoreType.DMA((max(used, 2),)),
            pltpu.SemaphoreType.DMA((used,)),
        ],
        compiler_params=pltpu.CompilerParams(
            collective_id=0, has_side_effects=True, vmem_limit_bytes=60 * 1024 * 1024
        ),
        name="transform",
    )(row_points, quad_weight, waves, coeffs, legendre, grid_factor[0])
    out = pl.pallas_call(
        functools.partial(output_kernel, span, group),
        out_shape=jax.ShapeDtypeStruct((chans, own), F32),
        in_specs=[SMEM] + [VMEM] * 2,
        out_specs=VMEM,
        scratch_shapes=[pltpu.VMEM((owners * used * per_owner, chans), F32)],
        compiler_params=PARAMS,
        name="output",
    )(wave_of_slot, table, back)
    if not gather:
        out = lax.psum(out, "lat")
    return out.reshape(2, levels, own)


def solution(mesh):
    return jax.shard_map(
        on_device,
        mesh=mesh,
        in_specs=(
            P(None, None, "wave"),
            P("lat", "wave"),
            P(),
            P("lat", None),
            P("lat", None),
            P("lat", None, None),
        ),
        out_specs=P(None, None, "wave"),
        check_vma=False,
    )
```

```python
import functools
import math

import jax
import jax.numpy as jnp
from jax import lax
from jax.experimental import pallas as pl
from jax.experimental.pallas import tpu as pltpu
from jax.sharding import PartitionSpec as P

TRUNC = 3999
M0 = 3488
MS = 512

F32 = jnp.float32
BF16 = jnp.bfloat16
MESH = pl.DeviceIdType.MESH
RADIX = 4
CHUNK = 512


def dot(a, b, ca, cb):
    return lax.dot_general(a, b, (((ca,), (cb,)), ((), ())), preferred_element_type=F32)


def column_bounds(waves, first_slot, span):
    slot = first_slot + lax.broadcasted_iota(jnp.int32, waves.shape, 0)
    pair = slot // 2
    length = TRUNC + 1 - waves
    low = slot % 2 == 0
    begin = jnp.where(low, pair * span, (pair + 1) * span - length)
    end = jnp.where(low, pair * span + length, (pair + 1) * span)
    return begin, end


def wave_column(waves_ref):
    row = waves_ref[...].astype(F32)
    return jnp.broadcast_to(row, (8, row.shape[1])).T[:, :1]


def pack_rows(leg_ref, pack_ref, packed_ref):
    group, own = leg_ref.shape
    length = packed_ref.shape[1]
    for piece in range(packed_ref.shape[0] // group):
        first, last = piece * length, min((piece + 1) * length, own)
        if last - first < length:
            pack_ref[group * piece : group * (piece + 1), :] = jnp.zeros((group, length), F32)
        pack_ref[group * piece : group * (piece + 1), : last - first] = leg_ref[
            :, first:last
        ].astype(F32)
    packed_ref[...] = pack_ref[...].astype(BF16)


def make_fourier(span, me, column_ref, spec_ref, leg_ref, acc_ref, out_ref):
    group, own = leg_ref.shape
    slots = acc_ref.shape[1]
    for first in range(0, slots, 8):
        c0 = first // 2 * span // 128 * 128
        c1 = min(-(-((first // 2 + 4) * span) // 128) * 128, own)
        waves = column_ref[pl.ds(pl.multiple_of(me * slots + first, 8), 8), :]
        begin, end = column_bounds(waves, first, span)
        column = c0 + lax.broadcasted_iota(jnp.int32, (8, c1 - c0), 1)
        inside = (column >= begin) & (column < end)
        rows = leg_ref[:, c0:c1].astype(F32)
        masked = jnp.concatenate(
            [jnp.where(inside, rows[r : r + 1, :], 0.0) for r in range(group)], 0
        ).astype(BF16)
        sums = dot(masked, spec_ref[:, c0:c1], 1, 1)
        for r in range(group):
            acc_ref[r, first : first + 8, :] = sums[8 * r : 8 * r + 8, :]
    for r in range(group):
        out_ref[r] = acc_ref[r].T.astype(BF16)


def shift_factors(quarter, row_ref, factor_ref):
    wide = row_ref.shape[1]
    row = row_ref[...]
    for t in range(RADIX):
        shifted = pltpu.roll(row, wide - t * quarter, 1) if t else row
        factor_ref[t : t + 1, :] = shifted[:, : factor_ref.shape[1]]


def output_kernel(
    span, group, waves_ref, leg_hbm, back_hbm, out_hbm, held_ref, leg_ref, back_ref, out_ref, sems
):
    me = lax.axis_index("wave")
    load_back = pltpu.make_async_copy(back_hbm, back_ref, sems.at[0])
    load_leg = pltpu.make_async_copy(leg_hbm, leg_ref, sems.at[1])
    load_back.start()
    load_leg.start()
    load_back.wait()
    groups, packed, length = leg_ref.shape
    own = out_ref.shape[1]
    rows, _, slots = back_ref.shape
    for r in range(rows):
        held_ref[slots * r : slots * (r + 1), :] = back_ref[r].astype(F32).T
    load_leg.wait()
    half = length // CHUNK // 2 * CHUNK
    stores = []

    def store(begin, end):
        for piece in range(packed // group):
            c0, c1 = piece * length + begin, min(piece * length + end, own)
            copy = pltpu.make_async_copy(
                out_ref.at[:, c0:c1], out_hbm.at[:, c0:c1], sems.at[2 + len(stores)]
            )
            copy.start()
            stores.append(copy)

    for at in range(0, length, CHUNK):
        if at == half:
            store(0, half)
        parts = [leg_ref[g, :, at : min(at + CHUNK, length)].astype(F32) for g in range(groups)]
        for piece in range(packed // group):
            c0 = piece * length + at
            c1 = min(c0 + CHUNK, (piece + 1) * length, own)
            if c1 <= c0:
                continue
            p0, p1 = c0 // span, (c1 - 1) // span + 1
            column = c0 + lax.broadcasted_iota(jnp.int32, (1, c1 - c0), 1)
            part = jnp.concatenate(
                [p[group * piece : group * (piece + 1), : c1 - c0] for p in parts], 0
            )
            masked, left = [], []
            for pair in range(p0, p1):
                split = pair * span + TRUNC + 1 - waves_ref[me * slots + 2 * pair]
                low = (column >= pair * span) & (column < split)
                high = (column >= split) & (column < (pair + 1) * span)
                masked.append(jnp.where(low, part, 0.0))
                masked.append(jnp.where(high, part, 0.0))
                left.append(held_ref[pl.ds(2 * pair, rows, stride=slots), :])
                left.append(held_ref[pl.ds(2 * pair + 1, rows, stride=slots), :])
            right = jnp.concatenate(masked, 0).astype(BF16)
            out_ref[:, c0:c1] = dot(jnp.concatenate(left, 0).astype(BF16), right, 0, 0)
    store(half, length)
    for copy in stores:
        copy.wait()


def sine_turns(v):
    y = v * v
    total = jnp.full_like(v, -((2 * math.pi) ** 11) / math.factorial(11))
    for power in (9, 7, 5, 3, 1):
        sign = 1.0 if power % 4 == 1 else -1.0
        total = total * y + sign * (2 * math.pi) ** power / math.factorial(power)
    return total * v


def angle_rows(count, start, width):
    row = lax.broadcasted_iota(jnp.int32, (32, width), 0)
    k = start + lax.broadcasted_iota(jnp.int32, (32, width), 1)
    mult = jnp.where(row < 8, M0 + 64 * row, jnp.where(row < 24, 4 * (row - 8), row - 24))
    product = (mult * k).astype(F32)
    inverse = 1.0 / count
    rest = product - count * jnp.round(product * inverse)
    turn = rest * inverse
    size = jnp.abs(turn)
    folded = jnp.minimum(size, 0.5 - size)
    return sine_turns(0.25 - size), jnp.where(turn < 0, -1.0, 1.0) * sine_turns(folded)


def halves(x):
    high = x.astype(BF16)
    return high, (x - high.astype(F32)).astype(BF16)


def order_matrix(waves):
    each = MS // RADIX
    column = lax.broadcasted_iota(jnp.int32, (MS, MS), 1)
    wave = M0 + RADIX * (column % each) + column // each
    return (waves == wave.astype(F32)).astype(F32).astype(BF16)


def transform_kernel(
    span, owners, groups, points_ref, weight_ref, waves_ref, spec_hbm, rows_hbm, grid_hbm,
    out_ref, table_ref, four_ref, factor_ref, leg_ref,
    sums_ref, row_ref, column_ref, pack_ref, spec_ref, rows_ref, grid_ref, sems, came_ref, leave_ref, acc_ref, high_ref, low_ref, turn_ref,
    send_four, recv_four, send_back, recv_back, send_leg, recv_leg,
):
    me, here = lax.axis_index("wave"), lax.axis_index("lat")
    lats = lax.axis_size("lat")
    base = here * owners if groups > 1 else 0
    offsets = [(w, l) for l in range(groups) for w in range(owners) if w or l]

    def peer(offset):
        return lax.rem(me + offset[0], owners), lax.rem(here + offset[1], lats)

    loads = [
        pltpu.make_async_copy(source, target, sems.at[i])
        for i, (source, target) in enumerate(
            ((rows_hbm, rows_ref), (spec_hbm, spec_ref), (grid_hbm, grid_ref))
        )
    ]
    for load in loads:
        load.start()
    barrier = pltpu.get_barrier_semaphore()
    for offset in offsets:
        pl.semaphore_signal(barrier, inc=1, device_id=peer(offset), device_id_type=MESH)
    column_ref[...] = wave_column(waves_ref).astype(jnp.int32)
    loads[0].wait()
    pack_rows(rows_ref, pack_ref, leg_ref)
    pl.semaphore_wait(barrier, len(offsets))

    def four_copy(step, to, owner):
        return pltpu.make_async_remote_copy(
            src_ref=four_ref.at[to],
            dst_ref=came_ref.at[owner],
            send_sem=send_four.at[step],
            recv_sem=recv_four.at[owner],
            device_id=(to, here),
            device_id_type=MESH,
        )

    sibling = here + 1 - 2 * lax.rem(here, 2)

    def leg_copy(at, source, row, to):
        return pltpu.make_async_remote_copy(
            src_ref=source,
            dst_ref=table_ref.at[row],
            send_sem=send_leg.at[at],
            recv_sem=recv_leg.at[row],
            device_id=(me, to),
            device_id_type=MESH,
        )

    if groups > 1:
        for step in range(2, groups, 2):
            leg_copy(step, leg_ref, here, lax.rem(here + step, lats)).start()
        leg_copy(0, leg_ref, here, sibling).start()
    loads[1].wait()
    make_fourier(span, me, column_ref, spec_ref, rows_ref, sums_ref, four_ref)
    for step in range(1, owners):
        four_copy(step, lax.rem(me + step, owners), me).start()
    came_ref[me] = four_ref[me]
    table_ref[here if groups > 1 else 0] = leg_ref[...]
    loads[2].wait()
    row_ref[...] = jnp.zeros_like(row_ref)
    row_ref[:, : grid_ref.shape[1]] = grid_ref[pl.ds(me, 1), :]
    shift_factors(points_ref[0, me] // RADIX, row_ref, factor_ref)

    count = points_ref[0, me].astype(F32)
    scale = weight_ref[0, me] / count
    quarter = count * 0.25
    levels = four_ref.shape[1] // 2
    each = MS // RADIX
    order = order_matrix(wave_column(waves_ref))

    def make_tables(index, carry):
        start = index * CHUNK
        cos, sin = angle_rows(count, start, CHUNK)
        cos_b, sin_b = cos[8:24], sin[8:24]
        table = jnp.concatenate(
            [cos[a : a + 1] * cos_b - sin[a : a + 1] * sin_b for a in range(8)]
            + [sin[a : a + 1] * cos_b + cos[a : a + 1] * sin_b for a in range(8)],
            0,
        )
        high, low = halves(table)
        high_ref[index] = high
        low_ref[index] = low
        turn_ref[index, :8] = cos[24:32]
        turn_ref[index, 8:] = sin[24:32]
        return carry

    chunks = factor_ref.shape[1] // CHUNK
    lax.fori_loop(0, chunks, make_tables, 0)
    acc_ref[...] = jnp.zeros_like(acc_ref)

    for step in range(1, owners):
        four_copy(step, lax.rem(me + step, owners), me).wait_send()
        owner = lax.rem(me + owners - step, owners)
        four_copy(step, owner, owner).wait_recv()
    arrived = jnp.concatenate([came_ref[w] for w in range(owners)], 1)
    ordered = dot(arrived, order, 1, 0)
    real = [ordered[:levels, each * c : each * (c + 1)] for c in range(RADIX)]
    imag = [ordered[levels:, each * c : each * (c + 1)] for c in range(RADIX)]
    left = jnp.concatenate(
        [jnp.concatenate([real[c], -imag[c]], 1) for c in range(RADIX)]
        + [jnp.concatenate([imag[c], real[c]], 1) for c in range(1, RADIX)],
        0,
    ).astype(BF16)

    def step(index, carry):
        start = index * CHUNK
        high, low = high_ref[index], low_ref[index]
        turns = turn_ref[index]
        mixed = dot(left, high, 1, 0) + dot(left, low, 1, 0)
        h = [mixed[levels * i : levels * (i + 1)] for i in range(7)]
        c1, c2, c3 = turns[1:2], turns[2:3], turns[3:4]
        s1, s2, s3 = turns[9:10], turns[10:11], turns[11:12]
        re1, im1 = h[1] * c1 - h[4] * s1, h[1] * s1 + h[4] * c1
        re2 = h[2] * c2 - h[5] * s2
        re3, im3 = h[3] * c3 - h[6] * s3, h[3] * s3 + h[6] * c3
        e, f, p, d = h[0] + re2, h[0] - re2, re1 + re3, im1 - im3
        k = (start + lax.broadcasted_iota(jnp.int32, (1, CHUNK), 1)).astype(F32)
        g = jnp.where(k < quarter, factor_ref[:, pl.ds(pl.multiple_of(start, CHUNK), CHUNK)], 0.0)
        q0, q1, q2, q3 = g[0:1] * (e + p), g[1:2] * (f - d), g[2:3] * (e - p), g[3:4] * (f + d)
        x, y = q0 - q2, q1 - q3
        u, v = q0 + q2, q1 + q3
        w = u - v
        turned = jnp.concatenate(
            [
                u + v,
                x * c1 - y * s1,
                w * c2,
                x * c3 + y * s3,
                -(x * s1 + y * c1),
                -(w * s2),
                y * c3 - x * s3,
            ],
            0,
        )
        t_high, t_low = halves(turned)
        acc_ref[...] += dot(t_high, high, 1, 1) + dot(t_low, high, 1, 1) + dot(t_high, low, 1, 1)
        return carry

    lax.fori_loop(0, chunks, step, 0)
    total = acc_ref[...] * scale
    on_cos = [total[levels * i : levels * (i + 1), :each] for i in range(7)]
    on_sin = [total[levels * i : levels * (i + 1), each:] for i in range(7)]
    back_re = jnp.concatenate(
        [on_cos[0]] + [on_cos[c] + on_sin[c + 3] for c in range(1, RADIX)], 1
    )
    back_im = jnp.concatenate(
        [-on_sin[0]] + [on_cos[c + 3] - on_sin[c] for c in range(1, RADIX)], 1
    )
    back = jnp.concatenate([back_re, back_im], 0).astype(BF16)
    by_slot = dot(back, order, 1, 1).astype(BF16)
    slots = four_ref.shape[2]
    for w in range(owners):
        leave_ref[w] = by_slot[:, slots * w : slots * (w + 1)]

    def back_copy(step, to, row):
        return pltpu.make_async_remote_copy(
            src_ref=leave_ref.at[to[0]],
            dst_ref=out_ref.at[row],
            send_sem=send_back.at[step],
            recv_sem=recv_back.at[row],
            device_id=to,
            device_id_type=MESH,
        )

    for step, offset in enumerate(offsets):
        back_copy(step, peer(offset), base + me).start()
    out_ref[base + me] = leave_ref[me]
    if groups > 1:
        for step in range(2, groups, 2):
            row = lax.rem(here + lats - step, lats)
            leg_copy(step, leg_ref, row, row).wait_recv()
            leg_copy(step + 1, table_ref.at[row], row, sibling).start()
        for step in range(0, groups, 2):
            leg_copy(step, leg_ref, here, sibling).wait_send()
            row = lax.rem(sibling + lats - step, lats)
            leg_copy(step, leg_ref, row, sibling).wait_recv()
        for step in range(2, groups, 2):
            row = lax.rem(here + lats - step, lats)
            leg_copy(step + 1, table_ref.at[row], row, sibling).wait_send()
    for step, offset in enumerate(offsets):
        back_copy(step, peer(offset), base + me).wait_send()
        source = lax.rem(me + owners - offset[0], owners), lax.rem(here + lats - offset[1], lats)
        row = source[1] * owners + source[0] if groups > 1 else source[0]
        back_copy(step, source, row).wait_recv()


VMEM = pl.BlockSpec(memory_space=pltpu.VMEM)
HBM = pl.BlockSpec(memory_space=pltpu.HBM)
SMEM = pl.BlockSpec(memory_space=pltpu.SMEM)


def on_device(spectral, legendre, wave_of_slot, row_points, quad_weight, grid_factor):
    levels = spectral.shape[1]
    chans = 2 * levels
    owners = lax.axis_size("wave")
    groups = lax.axis_size("lat")
    per_owner = MS // owners
    group, own = legendre.shape
    span = own // (per_owner // 2)
    gather = groups % 2 == 0 and groups * group * legendre.dtype.itemsize < 2 * chans * 4
    pieces = max(1, 16 // group)
    packed = -(-own // (pieces * 128)) * 128
    waves = wave_of_slot[None]
    coeffs = spectral.reshape(chans, own)
    length = grid_factor.shape[2]
    padded = -(-(length // RADIX) // CHUNK) * CHUNK
    wide = -(-length // 128) * 128
    used = groups if gather else 1
    others = owners * used - 1
    back, table = pl.pallas_call(
        functools.partial(transform_kernel, span, owners, used),
        out_shape=[
            jax.ShapeDtypeStruct((owners * used, chans, per_owner), BF16),
            jax.ShapeDtypeStruct((used, pieces * group, packed), BF16),
        ],
        in_specs=[SMEM] * 2 + [VMEM] + [HBM] * 3,
        out_specs=[VMEM] * 2,
        scratch_shapes=[
            pltpu.VMEM((group, chans, per_owner), BF16),
            pltpu.VMEM((RADIX, padded), F32),
            pltpu.VMEM((pieces * group, packed), BF16),
            pltpu.VMEM((group, per_owner, chans), F32),
            pltpu.VMEM((1, wide), F32),
            pltpu.VMEM((MS, 1), jnp.int32),
            pltpu.VMEM((pieces * group, packed), F32),
            pltpu.VMEM((chans, own), BF16),
            pltpu.VMEM((group, own), BF16),
            pltpu.VMEM(grid_factor.shape[1:], F32),
            pltpu.SemaphoreType.DMA((3,)),
            pltpu.VMEM((owners, chans, per_owner), BF16),
            pltpu.VMEM((owners, chans, per_owner), BF16),
            pltpu.VMEM((7 * levels, 2 * MS // RADIX), F32),
            pltpu.VMEM((padded // CHUNK, 2 * MS // RADIX, CHUNK), BF16),
            pltpu.VMEM((padded // CHUNK, 2 * MS // RADIX, CHUNK), BF16),
            pltpu.VMEM((padded // CHUNK, 16, CHUNK), F32),
            pltpu.SemaphoreType.DMA((owners,)),
            pltpu.SemaphoreType.DMA((owners,)),
            pltpu.SemaphoreType.DMA((others,)),
            pltpu.SemaphoreType.DMA((owners * used,)),
            pltpu.SemaphoreType.DMA((max(used, 2),)),
            pltpu.SemaphoreType.DMA((used,)),
        ],
        compiler_params=pltpu.CompilerParams(
            collective_id=0, has_side_effects=True, vmem_limit_bytes=60 * 1024 * 1024
        ),
        name="transform",
    )(row_points, quad_weight, waves, coeffs, legendre, grid_factor[0])
    out = pl.pallas_call(
        functools.partial(output_kernel, span, group),
        out_shape=jax.ShapeDtypeStruct((chans, own), F32),
        in_specs=[SMEM] + [HBM] * 2,
        out_specs=HBM,
        scratch_shapes=[
            pltpu.VMEM((owners * used * per_owner, chans), F32),
            pltpu.VMEM((used, pieces * group, packed), BF16),
            pltpu.VMEM((owners * used, chans, per_owner), BF16),
            pltpu.VMEM((chans, own), F32),
            pltpu.SemaphoreType.DMA((2 + 2 * pieces,)),
        ],
        compiler_params=pltpu.CompilerParams(vmem_limit_bytes=62 * 1024 * 1024),
        name="output",
    )(wave_of_slot, table, back)
    if not gather:
        out = lax.psum(out, "lat")
    return out.reshape(2, levels, own)


def solution(mesh):
    return jax.shard_map(
        on_device,
        mesh=mesh,
        in_specs=(
            P(None, None, "wave"),
            P("lat", "wave"),
            P(),
            P("lat", None),
            P("lat", None),
            P("lat", None, None),
        ),
        out_specs=P(None, None, "wave"),
        check_vma=False,
    )
```

```python
import functools
import math

import jax
import jax.numpy as jnp
from jax import lax
from jax.experimental import pallas as pl
from jax.experimental.pallas import tpu as pltpu
from jax.sharding import PartitionSpec as P

TRUNC = 3999
M0 = 3488
MS = 512

F32 = jnp.float32
BF16 = jnp.bfloat16
MESH = pl.DeviceIdType.MESH
RADIX = 4
CHUNK = 512


def dot(a, b, ca, cb):
    return lax.dot_general(a, b, (((ca,), (cb,)), ((), ())), preferred_element_type=F32)


def column_bounds(waves, first_slot, span):
    slot = first_slot + lax.broadcasted_iota(jnp.int32, waves.shape, 0)
    pair = slot // 2
    length = TRUNC + 1 - waves
    low = slot % 2 == 0
    begin = jnp.where(low, pair * span, (pair + 1) * span - length)
    end = jnp.where(low, pair * span + length, (pair + 1) * span)
    return begin, end


def wave_column(waves_ref):
    row = waves_ref[...].astype(F32)
    return jnp.broadcast_to(row, (8, row.shape[1])).T[:, :1]


def pack_rows(leg_ref, pack_ref, packed_ref):
    group, own = leg_ref.shape
    length = packed_ref.shape[1]
    for piece in range(packed_ref.shape[0] // group):
        first, last = piece * length, min((piece + 1) * length, own)
        if last - first < length:
            pack_ref[group * piece : group * (piece + 1), :] = jnp.zeros((group, length), F32)
        pack_ref[group * piece : group * (piece + 1), : last - first] = leg_ref[
            :, first:last
        ].astype(F32)
    packed_ref[...] = pack_ref[...].astype(BF16)


def make_fourier(span, me, column_ref, spec_ref, leg_ref, acc_ref, out_ref):
    group, own = leg_ref.shape
    slots = acc_ref.shape[1]
    for first in range(0, slots, 8):
        c0 = first // 2 * span // 128 * 128
        c1 = min(-(-((first // 2 + 4) * span) // 128) * 128, own)
        waves = column_ref[pl.ds(pl.multiple_of(me * slots + first, 8), 8), :]
        begin, end = column_bounds(waves, first, span)
        column = c0 + lax.broadcasted_iota(jnp.int32, (8, c1 - c0), 1)
        inside = (column >= begin) & (column < end)
        rows = leg_ref[:, c0:c1].astype(F32)
        masked = jnp.concatenate(
            [jnp.where(inside, rows[r : r + 1, :], 0.0) for r in range(group)], 0
        ).astype(BF16)
        sums = dot(masked, spec_ref[:, c0:c1], 1, 1)
        for r in range(group):
            acc_ref[r, first : first + 8, :] = sums[8 * r : 8 * r + 8, :]
    for r in range(group):
        out_ref[r] = acc_ref[r].T.astype(BF16)


def shift_factors(quarter, row_ref, factor_ref):
    wide = row_ref.shape[1]
    row = row_ref[...]
    for t in range(RADIX):
        shifted = pltpu.roll(row, wide - t * quarter, 1) if t else row
        factor_ref[t : t + 1, :] = shifted[:, : factor_ref.shape[1]]


def output_kernel(
    span, group, waves_ref, leg_hbm, back_hbm, out_hbm, held_ref, leg_ref, back_ref, out_ref, sems
):
    me = lax.axis_index("wave")
    load_back = pltpu.make_async_copy(back_hbm, back_ref, sems.at[0])
    load_leg = pltpu.make_async_copy(leg_hbm, leg_ref, sems.at[1])
    load_back.start()
    load_leg.start()
    load_back.wait()
    groups, packed, length = leg_ref.shape
    own = out_ref.shape[1]
    rows, _, slots = back_ref.shape
    for r in range(rows):
        held_ref[slots * r : slots * (r + 1), :] = back_ref[r].astype(F32).T
    load_leg.wait()
    half = length // CHUNK // 2 * CHUNK
    stores = []

    def store(begin, end):
        for piece in range(packed // group):
            c0, c1 = piece * length + begin, min(piece * length + end, own)
            copy = pltpu.make_async_copy(
                out_ref.at[:, c0:c1], out_hbm.at[:, c0:c1], sems.at[2 + len(stores)]
            )
            copy.start()
            stores.append(copy)

    for at in range(0, length, CHUNK):
        if at == half:
            store(0, half)
        parts = [leg_ref[g, :, at : min(at + CHUNK, length)].astype(F32) for g in range(groups)]
        for piece in range(packed // group):
            c0 = piece * length + at
            c1 = min(c0 + CHUNK, (piece + 1) * length, own)
            if c1 <= c0:
                continue
            p0, p1 = c0 // span, (c1 - 1) // span + 1
            column = c0 + lax.broadcasted_iota(jnp.int32, (1, c1 - c0), 1)
            part = jnp.concatenate(
                [p[group * piece : group * (piece + 1), : c1 - c0] for p in parts], 0
            )
            masked, left = [], []
            for pair in range(p0, p1):
                split = pair * span + TRUNC + 1 - waves_ref[me * slots + 2 * pair]
                low = (column >= pair * span) & (column < split)
                high = (column >= split) & (column < (pair + 1) * span)
                masked.append(jnp.where(low, part, 0.0))
                masked.append(jnp.where(high, part, 0.0))
                left.append(held_ref[pl.ds(2 * pair, rows, stride=slots), :])
                left.append(held_ref[pl.ds(2 * pair + 1, rows, stride=slots), :])
            right = jnp.concatenate(masked, 0).astype(BF16)
            out_ref[:, c0:c1] = dot(jnp.concatenate(left, 0).astype(BF16), right, 0, 0)
    store(half, length)
    for copy in stores:
        copy.wait()


def sine_turns(v):
    y = v * v
    total = jnp.full_like(v, -((2 * math.pi) ** 11) / math.factorial(11))
    for power in (9, 7, 5, 3, 1):
        sign = 1.0 if power % 4 == 1 else -1.0
        total = total * y + sign * (2 * math.pi) ** power / math.factorial(power)
    return total * v


def angle_rows(count, start, width):
    row = lax.broadcasted_iota(jnp.int32, (32, width), 0)
    k = start + lax.broadcasted_iota(jnp.int32, (32, width), 1)
    mult = jnp.where(row < 8, M0 + 64 * row, jnp.where(row < 24, 4 * (row - 8), row - 24))
    product = (mult * k).astype(F32)
    inverse = 1.0 / count
    rest = product - count * jnp.round(product * inverse)
    turn = rest * inverse
    size = jnp.abs(turn)
    folded = jnp.minimum(size, 0.5 - size)
    return sine_turns(0.25 - size), jnp.where(turn < 0, -1.0, 1.0) * sine_turns(folded)


def halves(x):
    high = x.astype(BF16)
    return high, (x - high.astype(F32)).astype(BF16)


def order_matrix(waves):
    each = MS // RADIX
    column = lax.broadcasted_iota(jnp.int32, (MS, MS), 1)
    wave = M0 + RADIX * (column % each) + column // each
    return (waves == wave.astype(F32)).astype(F32).astype(BF16)


def transform_kernel(
    span, owners, groups, points_ref, weight_ref, waves_ref, spec_hbm, rows_hbm, grid_hbm,
    out_ref, table_ref, four_ref, factor_ref, leg_ref,
    sums_ref, row_ref, column_ref, pack_ref, spec_ref, rows_ref, grid_ref, sems, came_ref, leave_ref, acc_ref, high_ref, low_ref, turn_ref,
    send_four, recv_four, send_back, recv_back, send_leg, recv_leg,
):
    me, here = lax.axis_index("wave"), lax.axis_index("lat")
    lats = lax.axis_size("lat")
    base = here * owners if groups > 1 else 0
    offsets = [(w, l) for l in range(groups) for w in range(owners) if w or l]

    def peer(offset):
        return lax.rem(me + offset[0], owners), lax.rem(here + offset[1], lats)

    loads = [
        pltpu.make_async_copy(source, target, sems.at[i])
        for i, (source, target) in enumerate(
            ((rows_hbm, rows_ref), (spec_hbm, spec_ref), (grid_hbm, grid_ref))
        )
    ]
    for load in loads:
        load.start()
    barrier = pltpu.get_barrier_semaphore()
    for offset in offsets:
        pl.semaphore_signal(barrier, inc=1, device_id=peer(offset), device_id_type=MESH)
    column_ref[...] = wave_column(waves_ref).astype(jnp.int32)
    loads[0].wait()
    pack_rows(rows_ref, pack_ref, leg_ref)
    pl.semaphore_wait(barrier, len(offsets))

    def four_copy(step, to, owner):
        return pltpu.make_async_remote_copy(
            src_ref=four_ref.at[to],
            dst_ref=came_ref.at[owner],
            send_sem=send_four.at[step],
            recv_sem=recv_four.at[owner],
            device_id=(to, here),
            device_id_type=MESH,
        )

    sibling = here + 1 - 2 * lax.rem(here, 2)

    def leg_copy(at, source, row, to):
        return pltpu.make_async_remote_copy(
            src_ref=source,
            dst_ref=table_ref.at[row],
            send_sem=send_leg.at[at],
            recv_sem=recv_leg.at[row],
            device_id=(me, to),
            device_id_type=MESH,
        )

    if groups > 1:
        for step in range(2, groups, 2):
            leg_copy(step, leg_ref, here, lax.rem(here + step, lats)).start()
        leg_copy(0, leg_ref, here, sibling).start()
    loads[1].wait()
    make_fourier(span, me, column_ref, spec_ref, rows_ref, sums_ref, four_ref)
    for step in range(1, owners):
        four_copy(step, lax.rem(me + step, owners), me).start()
    came_ref[me] = four_ref[me]
    table_ref[here if groups > 1 else 0] = leg_ref[...]
    loads[2].wait()
    row_ref[...] = jnp.zeros_like(row_ref)
    row_ref[:, : grid_ref.shape[1]] = grid_ref[pl.ds(me, 1), :]
    shift_factors(points_ref[0, me] // RADIX, row_ref, factor_ref)

    count = points_ref[0, me].astype(F32)
    scale = weight_ref[0, me] / count
    quarter = count * 0.25
    levels = four_ref.shape[1] // 2
    each = MS // RADIX
    order = order_matrix(wave_column(waves_ref))

    def make_tables(index, carry):
        start = index * CHUNK
        cos, sin = angle_rows(count, start, CHUNK)
        cos_b, sin_b = cos[8:24], sin[8:24]
        table = jnp.concatenate(
            [cos[a : a + 1] * cos_b - sin[a : a + 1] * sin_b for a in range(8)]
            + [sin[a : a + 1] * cos_b + cos[a : a + 1] * sin_b for a in range(8)],
            0,
        )
        high, low = halves(table)
        high_ref[index] = high
        low_ref[index] = low
        turn_ref[index, :8] = cos[24:32]
        turn_ref[index, 8:] = sin[24:32]
        return carry

    chunks = factor_ref.shape[1] // CHUNK
    lax.fori_loop(0, chunks, make_tables, 0)
    acc_ref[...] = jnp.zeros_like(acc_ref)

    for step in range(1, owners):
        four_copy(step, lax.rem(me + step, owners), me).wait_send()
        owner = lax.rem(me + owners - step, owners)
        four_copy(step, owner, owner).wait_recv()
    arrived = jnp.concatenate([came_ref[w] for w in range(owners)], 1)
    ordered = dot(arrived, order, 1, 0)
    real = [ordered[:levels, each * c : each * (c + 1)] for c in range(RADIX)]
    imag = [ordered[levels:, each * c : each * (c + 1)] for c in range(RADIX)]
    left = jnp.concatenate(
        [jnp.concatenate([real[c], -imag[c]], 1) for c in range(RADIX)]
        + [jnp.concatenate([imag[c], real[c]], 1) for c in range(1, RADIX)],
        0,
    ).astype(BF16)

    def step(index, carry):
        start = index * CHUNK
        high, low = high_ref[index], low_ref[index]
        turns = turn_ref[index]
        mixed = dot(left, high, 1, 0) + dot(left, low, 1, 0)
        h = [mixed[levels * i : levels * (i + 1)] for i in range(7)]
        c1, c2, c3 = turns[1:2], turns[2:3], turns[3:4]
        s1, s2, s3 = turns[9:10], turns[10:11], turns[11:12]
        re1, im1 = h[1] * c1 - h[4] * s1, h[1] * s1 + h[4] * c1
        re2 = h[2] * c2 - h[5] * s2
        re3, im3 = h[3] * c3 - h[6] * s3, h[3] * s3 + h[6] * c3
        e, f, p, d = h[0] + re2, h[0] - re2, re1 + re3, im1 - im3
        k = (start + lax.broadcasted_iota(jnp.int32, (1, CHUNK), 1)).astype(F32)
        g = jnp.where(k < quarter, factor_ref[:, pl.ds(pl.multiple_of(start, CHUNK), CHUNK)], 0.0)
        q0, q1, q2, q3 = g[0:1] * (e + p), g[1:2] * (f - d), g[2:3] * (e - p), g[3:4] * (f + d)
        x, y = q0 - q2, q1 - q3
        u, v = q0 + q2, q1 + q3
        w = u - v
        turned = jnp.concatenate(
            [
                u + v,
                x * c1 - y * s1,
                w * c2,
                x * c3 + y * s3,
                -(x * s1 + y * c1),
                -(w * s2),
                y * c3 - x * s3,
            ],
            0,
        )
        t_high, t_low = halves(turned)
        acc_ref[...] += dot(t_high, high, 1, 1) + dot(t_low, high, 1, 1) + dot(t_high, low, 1, 1)
        return carry

    lax.fori_loop(0, chunks, step, 0)
    if groups > 1:
        for hop in range(2, groups, 2):
            row = lax.rem(here + lats - hop, lats)
            leg_copy(hop, leg_ref, row, row).wait_recv()
            leg_copy(hop + 1, table_ref.at[row], row, sibling).start()
    total = acc_ref[...] * scale
    on_cos = [total[levels * i : levels * (i + 1), :each] for i in range(7)]
    on_sin = [total[levels * i : levels * (i + 1), each:] for i in range(7)]
    back_re = jnp.concatenate(
        [on_cos[0]] + [on_cos[c] + on_sin[c + 3] for c in range(1, RADIX)], 1
    )
    back_im = jnp.concatenate(
        [-on_sin[0]] + [on_cos[c + 3] - on_sin[c] for c in range(1, RADIX)], 1
    )
    back = jnp.concatenate([back_re, back_im], 0).astype(BF16)
    by_slot = dot(back, order, 1, 1).astype(BF16)
    slots = four_ref.shape[2]
    for w in range(owners):
        leave_ref[w] = by_slot[:, slots * w : slots * (w + 1)]

    def back_copy(step, to, row):
        return pltpu.make_async_remote_copy(
            src_ref=leave_ref.at[to[0]],
            dst_ref=out_ref.at[row],
            send_sem=send_back.at[step],
            recv_sem=recv_back.at[row],
            device_id=to,
            device_id_type=MESH,
        )

    for step, offset in enumerate(offsets):
        back_copy(step, peer(offset), base + me).start()
    out_ref[base + me] = leave_ref[me]
    if groups > 1:
        for step in range(0, groups, 2):
            leg_copy(step, leg_ref, here, sibling).wait_send()
            row = lax.rem(sibling + lats - step, lats)
            leg_copy(step, leg_ref, row, sibling).wait_recv()
        for step in range(2, groups, 2):
            row = lax.rem(here + lats - step, lats)
            leg_copy(step + 1, table_ref.at[row], row, sibling).wait_send()
    for step, offset in enumerate(offsets):
        back_copy(step, peer(offset), base + me).wait_send()
        source = lax.rem(me + owners - offset[0], owners), lax.rem(here + lats - offset[1], lats)
        row = source[1] * owners + source[0] if groups > 1 else source[0]
        back_copy(step, source, row).wait_recv()


VMEM = pl.BlockSpec(memory_space=pltpu.VMEM)
HBM = pl.BlockSpec(memory_space=pltpu.HBM)
SMEM = pl.BlockSpec(memory_space=pltpu.SMEM)


def on_device(spectral, legendre, wave_of_slot, row_points, quad_weight, grid_factor):
    levels = spectral.shape[1]
    chans = 2 * levels
    owners = lax.axis_size("wave")
    groups = lax.axis_size("lat")
    per_owner = MS // owners
    group, own = legendre.shape
    span = own // (per_owner // 2)
    gather = groups % 2 == 0 and groups * group * legendre.dtype.itemsize < 2 * chans * 4
    pieces = max(1, 16 // group)
    packed = -(-own // (pieces * 128)) * 128
    waves = wave_of_slot[None]
    coeffs = spectral.reshape(chans, own)
    length = grid_factor.shape[2]
    padded = -(-(length // RADIX) // CHUNK) * CHUNK
    wide = -(-length // 128) * 128
    used = groups if gather else 1
    others = owners * used - 1
    back, table = pl.pallas_call(
        functools.partial(transform_kernel, span, owners, used),
        out_shape=[
            jax.ShapeDtypeStruct((owners * used, chans, per_owner), BF16),
            jax.ShapeDtypeStruct((used, pieces * group, packed), BF16),
        ],
        in_specs=[SMEM] * 2 + [VMEM] + [HBM] * 3,
        out_specs=[VMEM] * 2,
        scratch_shapes=[
            pltpu.VMEM((group, chans, per_owner), BF16),
            pltpu.VMEM((RADIX, padded), F32),
            pltpu.VMEM((pieces * group, packed), BF16),
            pltpu.VMEM((group, per_owner, chans), F32),
            pltpu.VMEM((1, wide), F32),
            pltpu.VMEM((MS, 1), jnp.int32),
            pltpu.VMEM((pieces * group, packed), F32),
            pltpu.VMEM((chans, own), BF16),
            pltpu.VMEM((group, own), BF16),
            pltpu.VMEM(grid_factor.shape[1:], F32),
            pltpu.SemaphoreType.DMA((3,)),
            pltpu.VMEM((owners, chans, per_owner), BF16),
            pltpu.VMEM((owners, chans, per_owner), BF16),
            pltpu.VMEM((7 * levels, 2 * MS // RADIX), F32),
            pltpu.VMEM((padded // CHUNK, 2 * MS // RADIX, CHUNK), BF16),
            pltpu.VMEM((padded // CHUNK, 2 * MS // RADIX, CHUNK), BF16),
            pltpu.VMEM((padded // CHUNK, 16, CHUNK), F32),
            pltpu.SemaphoreType.DMA((owners,)),
            pltpu.SemaphoreType.DMA((owners,)),
            pltpu.SemaphoreType.DMA((others,)),
            pltpu.SemaphoreType.DMA((owners * used,)),
            pltpu.SemaphoreType.DMA((max(used, 2),)),
            pltpu.SemaphoreType.DMA((used,)),
        ],
        compiler_params=pltpu.CompilerParams(
            collective_id=0, has_side_effects=True, vmem_limit_bytes=60 * 1024 * 1024
        ),
        name="transform",
    )(row_points, quad_weight, waves, coeffs, legendre, grid_factor[0])
    out = pl.pallas_call(
        functools.partial(output_kernel, span, group),
        out_shape=jax.ShapeDtypeStruct((chans, own), F32),
        in_specs=[SMEM] + [HBM] * 2,
        out_specs=HBM,
        scratch_shapes=[
            pltpu.VMEM((owners * used * per_owner, chans), F32),
            pltpu.VMEM((used, pieces * group, packed), BF16),
            pltpu.VMEM((owners * used, chans, per_owner), BF16),
            pltpu.VMEM((chans, own), F32),
            pltpu.SemaphoreType.DMA((2 + 2 * pieces,)),
        ],
        compiler_params=pltpu.CompilerParams(vmem_limit_bytes=62 * 1024 * 1024),
        name="output",
    )(wave_of_slot, table, back)
    if not gather:
        out = lax.psum(out, "lat")
    return out.reshape(2, levels, own)


def solution(mesh):
    return jax.shard_map(
        on_device,
        mesh=mesh,
        in_specs=(
            P(None, None, "wave"),
            P("lat", "wave"),
            P(),
            P("lat", None),
            P("lat", None),
            P("lat", None, None),
        ),
        out_specs=P(None, None, "wave"),
        check_vma=False,
    )
```
